512 devices in a mesh: src: 16 (over x, z_hi), shard: 32 (over y, z_lo, core).
Axes of the slice: x: 4, y: 4, z: 16 (z_hi: 4, z_lo: 4; z = z_hi * 4 + z_lo), core: 2. Of those that a mesh axis runs over, the one named last changes fastest.
Arguments:
- weights: bfloat16 [16, 4096, 14848], P('src', None, 'shard'), may hold values from -0.09375 to 0.09375
- calib_pool: bfloat16 [512, 4096], P(('src', 'shard')), may hold values from -6 to 6
- cand_index: int32 [4, 16], replicated, may hold values from 0 to 15
- coef_table: float32 [16], replicated, may hold values from 0.05 to 0.6
- row_ids: int32 [512], replicated, may hold values from 0 to 511
Outputs:
- acts: bfloat16 [512, 4, 14848], P('src', None, 'shard')
The draws below stay inside these ranges and needn't reach their ends.
All inputs are finite; a program needn't handle non-finite values.
Results may differ from the reference program's by a relative error of at most 0.001.
Values may be sent and summed in bfloat16 or wider, within the bound.
No kernel may reach another device: no remote copies, remote signals or barrier semaphores. Data moves between devices by JAX's collectives and lax.ppermute only.
A program may use at most 128 MiB of HBM per device.

```python
import math
import jax
import jax.numpy as jnp
from jax import lax

D = 4096
FFW = 14848
CANDS = 4
TABLE = 16
ROWS = 512
SOURCES = 16
POOL = 512


def set_ends(entries, rng, low, high):
    extent = entries.shape
    index_at = [jax.random.randint(jax.random.fold_in(rng, axis), (), 0, extent[axis]) for axis in range(len(extent))]
    entries = entries.at[tuple(index_at)].set(low)
    longest = extent.index(max(extent))
    index_at[longest] = (index_at[longest] + 1) % extent[longest]
    return entries.at[tuple(index_at)].set(high)


def steps_of(stream_key, dims, shards, low, high):
    level, own = 1.0, jax.random.fold_in(stream_key, 6)
    for axis_at, shards_of in shards:
        heights = jnp.exp(jax.random.uniform(jax.random.fold_in(own, axis_at), (shards_of,), jnp.float32, low / len(shards), high / len(shards)))
        level = level * jnp.repeat(heights, dims[axis_at] // shards_of).reshape([-1 if axis == axis_at else 1 for axis in range(len(dims))])
    return level


def gaussian(own_key, dims, deviation, reach, shards=(), kind=jnp.bfloat16):
    gain = steps_of(own_key, dims, shards, -0.22, 0.18) if shards else 1.0
    array = jax.random.normal(own_key, dims, jnp.float32) * deviation * gain
    return jnp.minimum(jnp.maximum(array, -reach), reach).astype(kind)


def setup_inputs(seed: int = 0) -> dict:
    key_list = jax.random.split(jax.random.key(seed), 6)
    return {
        "weights": gaussian(key_list[0], (SOURCES, D, FFW), D ** -0.5, 0.09375, ((0, 16), (2, 32))),
        "calib_pool": gaussian(key_list[1], (POOL, D), 1.0, 6.0, ((0, 512),)),
        "cand_index": set_ends(jax.random.randint(key_list[2], (CANDS, SOURCES), 0, TABLE), jax.random.fold_in(key_list[2], 1), 0, TABLE - 1).astype(jnp.int32),
        "coef_table": jnp.clip(jnp.exp(jax.random.uniform(key_list[3], (TABLE,), jnp.float32, math.log(0.05), math.log(0.6))), 0.05, 0.6),
        "row_ids": set_ends(jax.random.randint(key_list[4], (ROWS,), 0, POOL), jax.random.fold_in(key_list[4], 1), 0, POOL - 1).astype(jnp.int32),
    }


def reference(weights, calib_pool, cand_index, coef_table, row_ids):
    coefficient = coef_table[cand_index]
    calib_rows = calib_pool[row_ids]

    def add_source(running, inputs):
        weight_piece, column = inputs
        partial_value = jnp.dot(calib_rows, weight_piece, preferred_element_type=jnp.float32)
        return running + partial_value[:, None, :] * column[None, :, None], None

    start_value = jnp.zeros((ROWS, CANDS, FFW), jnp.float32)
    running, unused = lax.scan(add_source, start_value, (weights, jnp.transpose(coefficient)))
    return running.astype(jnp.bfloat16)
```

```python
import jax
import jax.numpy as jnp
from jax import lax
from jax.sharding import Mesh, PartitionSpec as P

BF16, F32, I16, I32 = jnp.bfloat16, jnp.float32, jnp.int16, jnp.int32
LANES = 512
TOP = 32767.0


def spread(block, axes, count):
    copies = jnp.broadcast_to(block[None], (count,) + block.shape)
    return lax.all_to_all(copies, axes, 0, 0)


def encode(partial):
    top = jnp.max(jnp.abs(partial), axis=1, keepdims=True)
    power = jnp.clip(jnp.floor(jnp.log2(top)), -80.0, 80.0)
    mantissa = jnp.ceil(top * jnp.exp2(-power) * 8192.0) + 1.0
    step = mantissa * jnp.exp2(power) * (1.0 / (8192.0 * TOP))
    codes = jnp.clip(jnp.round(partial / step), -TOP, TOP)
    rows, width = partial.shape
    column = lax.broadcasted_iota(I32, (rows, LANES), 1)
    codes = jnp.pad(codes, ((0, 0), (0, LANES - width)))
    codes = jnp.where(column == width, mantissa, codes)
    return jnp.where(column == width + 1, power, codes)


def on_device(weights, calib_pool, cand_index, coef_table, row_ids):
    core = lax.axis_index("c")
    own = spread(calib_pool.reshape(32, 128), ("zh", "zl"), 16).reshape(16, 4096)
    own = spread(own, ("x", "y"), 16).reshape(256, 4096)
    other = lax.ppermute(own, "c", [(0, 1), (1, 0)])
    w_piece = weights[0]
    mine = jnp.dot(own, w_piece, preferred_element_type=F32)
    others = jnp.dot(other, w_piece, preferred_element_type=F32)
    partial = jnp.concatenate([mine, others], axis=0)
    width = partial.shape[1]

    codes = encode(partial)
    high = jnp.floor(codes * (1.0 / 256.0))
    low = codes - high * 256.0
    x, zh, y, zl, c = (row_ids >> 7) & 3, (row_ids >> 5) & 3, (row_ids >> 3) & 3, (row_ids >> 1) & 3, row_ids & 1
    place = ((x * 4 + y) * 4 + zh) * 4 + zl + jnp.where(c == core, 0, 256)
    pick = (place[:, None] == lax.broadcasted_iota(I32, (512, 512), 1)).astype(BF16)
    high = jnp.dot(pick, high.astype(BF16), preferred_element_type=F32)
    low = jnp.dot(pick, low.astype(BF16), preferred_element_type=F32)
    sent = (high * 256.0 + low).astype(I32).astype(I16)
    got = lax.all_to_all(sent, ("x", "zh"), 0, 0, tiled=True).reshape(16, 32, LANES)

    entries = jnp.arange(coef_table.shape[0], dtype=I32)
    onehot = (cand_index[:, :, None] == entries[None, None, :]).astype(F32)
    coefficient = jnp.sum(onehot * coef_table[None, None, :], axis=2)
    got = got.astype(F32)
    step = got[:, :, width] * jnp.exp2(got[:, :, width + 1]) * (1.0 / (8192.0 * TOP))
    factor = coefficient.T[:, None, :] * step[:, :, None]
    acts = jnp.sum(factor[:, :, :, None] * got[:, :, None, :width], axis=0)
    return acts.astype(BF16)


def solution(mesh):
    fine = Mesh(mesh.devices.reshape(4, 4, 4, 4, 2), ("x", "zh", "y", "zl", "c"))
    src, shard = ("x", "zh"), ("y", "zl", "c")
    placed = (P(src, None, shard), P(src + shard, None), P(), P(), P())
    return jax.shard_map(on_device, mesh=fine, in_specs=placed, out_specs=P(src, None, shard), check_vma=False)
```

```python
import jax
import jax.numpy as jnp
from jax import lax
from jax.sharding import Mesh, PartitionSpec as P

BF16, F32, I16, I32 = jnp.bfloat16, jnp.float32, jnp.int16, jnp.int32
LANES = 512
TOP = 32767.0


def spread(block, axes, count, groups=None):
    copies = jnp.broadcast_to(block[None], (count,) + block.shape)
    return lax.all_to_all(copies, axes, 0, 0, axis_index_groups=groups)


def lines(along):
    def at(x, y, role):
        return (x * 4 + y) * 2 + (role + x + y) % 2

    return [[at(i, j, along) for j in range(4)] for i in range(4)] + [
        [at(i, j, 1 - along) for i in range(4)] for j in range(4)
    ]


def encode(partial):
    top = jnp.max(jnp.abs(partial), axis=1, keepdims=True)
    power = jnp.clip(jnp.floor(jnp.log2(top)), -80.0, 80.0)
    mantissa = jnp.ceil(top * jnp.exp2(-power) * 8192.0) + 1.0
    step = mantissa * jnp.exp2(power) * (1.0 / (8192.0 * TOP))
    codes = jnp.clip(jnp.round(partial / step), -TOP, TOP)
    rows, width = partial.shape
    column = lax.broadcasted_iota(I32, (rows, LANES), 1)
    codes = jnp.pad(codes, ((0, 0), (0, LANES - width)))
    codes = jnp.where(column == width, mantissa, codes)
    return jnp.where(column == width + 1, power, codes)


def on_device(weights, calib_pool, cand_index, coef_table, row_ids):
    core = lax.axis_index("c")
    role = (core + lax.axis_index("x") + lax.axis_index("y")) % 2
    own = spread(calib_pool.reshape(32, 128), ("zh", "zl"), 16).reshape(16, 4096)
    own = spread(own, ("x", "y", "c"), 4, lines(0)).reshape(64, 4096)
    own = spread(own, ("x", "y", "c"), 4, lines(1)).reshape(256, 4096)
    other = lax.ppermute(own, "c", [(0, 1), (1, 0)])
    w_piece = weights[0]
    mine = jnp.dot(own, w_piece, preferred_element_type=F32)
    others = jnp.dot(other, w_piece, preferred_element_type=F32)
    partial = jnp.concatenate([mine, others], axis=0)
    width = partial.shape[1]

    codes = encode(partial)
    high = jnp.floor(codes * (1.0 / 256.0))
    low = codes - high * 256.0
    x, zh, y, zl, c = (row_ids >> 7) & 3, (row_ids >> 5) & 3, (row_ids >> 3) & 3, (row_ids >> 1) & 3, row_ids & 1
    its_role = (c + x + y) & 1
    place = jnp.where(its_role == 0, x * 4 + y, y * 4 + x) * 16 + zh * 4 + zl + jnp.where(its_role == role, 0, 256)
    pick = (place[:, None] == lax.broadcasted_iota(I32, (512, 512), 1)).astype(BF16)
    high = jnp.dot(pick, high.astype(BF16), preferred_element_type=F32)
    low = jnp.dot(pick, low.astype(BF16), preferred_element_type=F32)
    sent = (high * 256.0 + low).astype(I32).astype(I16)
    got = lax.all_to_all(sent, ("x", "zh"), 0, 0, tiled=True).reshape(16, 32, LANES)

    entries = jnp.arange(coef_table.shape[0], dtype=I32)
    onehot = (cand_index[:, :, None] == entries[None, None, :]).astype(F32)
    coefficient = jnp.sum(onehot * coef_table[None, None, :], axis=2)
    got = got.astype(F32)
    step = got[:, :, width] * jnp.exp2(got[:, :, width + 1]) * (1.0 / (8192.0 * TOP))
    factor = coefficient.T[:, None, :] * step[:, :, None]
    acts = jnp.sum(factor[:, :, :, None] * got[:, :, None, :width], axis=0)
    return acts.astype(BF16)


def solution(mesh):
    fine = Mesh(mesh.devices.reshape(4, 4, 4, 4, 2), ("x", "zh", "y", "zl", "c"))
    src, shard = ("x", "zh"), ("y", "zl", "c")
    placed = (P(src, None, shard), P(src + shard, None), P(), P(), P())
    return jax.shard_map(on_device, mesh=fine, in_specs=placed, out_specs=P(src, None, shard), check_vma=False)
```

```python
import jax
import jax.numpy as jnp
from jax import lax
from jax.experimental import pallas as pl
from jax.experimental.pallas import tpu as pltpu
from jax.sharding import Mesh, PartitionSpec as P

BF16, F32, I16, I32 = jnp.bfloat16, jnp.float32, jnp.int16, jnp.int32
LANES = 512
TOP = 32767.0
SHIFTS = (2, 1, 3)
DEPTH = 512


def spread(block, axes, count):
    copies = jnp.broadcast_to(block[None], (count,) + block.shape)
    return lax.all_to_all(copies, axes, 0, 0)


def shifted(block, along, shift):
    def at(x, y, c):
        return (x % 4 * 4 + y % 4) * 2 + c

    pairs = [
        (at(x, y, c), at(x, y + shift, c) if c == along else at(x + shift, y, c))
        for x in range(4)
        for y in range(4)
        for c in range(2)
    ]
    return lax.ppermute(block, ("x", "y", "c"), pairs)


def swapped(block):
    return lax.ppermute(block, "c", [(0, 1), (1, 0)])


def product(rows, w_ref):
    total = None
    for at in range(0, w_ref.shape[1], DEPTH):
        block = jnp.concatenate([r[:, at : at + DEPTH] for r in rows], axis=0)
        term = lax.dot_general(
            block, w_ref[:, at : at + DEPTH], (((1,), (1,)), ((), ())), preferred_element_type=F32
        )
        total = term if total is None else total + term
    return total


def first_kernel(a, b, c, d, w_ref, out_ref):
    out_ref[...] = product((a, b, c, d), w_ref)


def encode(partial):
    rows, width = partial.shape
    top = jnp.max(jnp.abs(partial), axis=1, keepdims=True)
    power = jnp.clip(jnp.floor(jnp.log2(top)), -80.0, 80.0)
    mantissa = jnp.ceil(top * jnp.exp2(-power) * 8192.0) + 1.0
    step = mantissa * jnp.exp2(power) * (1.0 / (8192.0 * TOP))
    codes = jnp.clip(jnp.round(partial * (1.0 / step)), -TOP, TOP)
    codes = jnp.concatenate([codes, jnp.zeros((rows, LANES - width), F32)], axis=1)
    column = lax.broadcasted_iota(I32, (rows, LANES), 1)
    codes = jnp.where(column == width, mantissa, codes)
    codes = jnp.where(column == width + 1, power, codes)
    high = jnp.floor(codes * (1.0 / 256.0))
    return high.astype(BF16), (codes - high * 256.0).astype(BF16)


def second_kernel(a, b, c, d, w_ref, first_ref, place_ref, out_ref, high_ref, low_ref):
    half = first_ref.shape[0]
    high_ref[:half], low_ref[:half] = encode(first_ref[...])
    high_ref[half:], low_ref[half:] = encode(product((a, b, c, d), w_ref))
    for at in range(0, 512, 256):
        column = lax.broadcasted_iota(I32, (256, 512), 1)
        pick = jnp.where(place_ref[at : at + 256] == column, 1.0, 0.0).astype(BF16)
        high = jnp.dot(pick, high_ref[...], preferred_element_type=F32)
        low = jnp.dot(pick, low_ref[...], preferred_element_type=F32)
        out_ref[at : at + 256] = (high * 256.0 + low).astype(I32).astype(I16)


def on_device(weights, calib_pool, cand_index, coef_table, row_ids):
    core, my_x, my_y = lax.axis_index("c"), lax.axis_index("x"), lax.axis_index("y")
    w_piece = weights[0].T
    start = spread(calib_pool.reshape(32, 128), ("zh", "zl"), 16).reshape(16, 4096)
    start = jnp.concatenate([start] + [shifted(start, 0, k) for k in (1, 2, 3)], axis=0)
    own = [start] + [shifted(start, 1, k) for k in SHIFTS]
    other = [swapped(piece) for piece in own]

    width = w_piece.shape[0]
    params = pltpu.CompilerParams(vmem_limit_bytes=40 * 2**20)
    cost = pl.CostEstimate(flops=2 * 256 * 4096 * width, bytes_accessed=6 * 2**20, transcendentals=0)
    first = pl.pallas_call(
        first_kernel,
        out_shape=jax.ShapeDtypeStruct((256, width), F32),
        compiler_params=params,
        cost_estimate=cost,
        name="first",
    )(own[0], own[1], other[0], other[1], w_piece)

    x, zh, y, zl, c = (row_ids >> 7) & 3, (row_ids >> 5) & 3, (row_ids >> 3) & 3, (row_ids >> 1) & 3, row_ids & 1
    back_x, back_y = (my_x - x) & 3, (my_y - y) & 3
    inner, outer = jnp.where(c == 0, back_y, back_x), jnp.where(c == 0, back_x, back_y)
    slot = jnp.where(outer == 0, 0, jnp.where(outer == 2, 1, jnp.where(outer == 1, 2, 3)))
    place = (slot >> 1) * 256 + jnp.where(c == core, 0, 128) + (slot & 1) * 64 + inner * 16 + zh * 4 + zl

    sent = pl.pallas_call(
        second_kernel,
        out_shape=jax.ShapeDtypeStruct((512, LANES), I16),
        scratch_shapes=[pltpu.VMEM((512, LANES), BF16)] * 2,
        compiler_params=params,
        cost_estimate=cost,
        name="second",
    )(own[2], own[3], other[2], other[3], w_piece, first, place[:, None])
    got = lax.all_to_all(sent, ("x", "zh"), 0, 0, tiled=True).reshape(16, 32, LANES)

    entries = jnp.arange(coef_table.shape[0], dtype=I32)
    onehot = (cand_index[:, :, None] == entries[None, None, :]).astype(F32)
    coefficient = jnp.sum(onehot * coef_table[None, None, :], axis=2)
    got = got.astype(F32)
    step = got[:, :, width] * jnp.exp2(got[:, :, width + 1]) * (1.0 / (8192.0 * TOP))
    factor = coefficient.T[:, None, :] * step[:, :, None]
    acts = jnp.sum(factor[:, :, :, None] * got[:, :, None, :width], axis=0)
    return acts.astype(BF16)


def solution(mesh):
    fine = Mesh(mesh.devices.reshape(4, 4, 4, 4, 2), ("x", "zh", "y", "zl", "c"))
    src, shard = ("x", "zh"), ("y", "zl", "c")
    placed = (P(src, None, shard), P(src + shard, None), P(), P(), P())
    return jax.shard_map(on_device, mesh=fine, in_specs=placed, out_specs=P(src, None, shard), check_vma=False)
```

```python
import jax
import jax.numpy as jnp
from jax import lax
from jax.experimental import pallas as pl
from jax.experimental.pallas import tpu as pltpu
from jax.sharding import Mesh, PartitionSpec as P

BF16, F32, I16, I32 = jnp.bfloat16, jnp.float32, jnp.int16, jnp.int32
LANES = 512
TOP = 32767.0
AXES = ("x", "zh", "y", "zl", "c")


def spread(block, axes, groups):
    copies = jnp.broadcast_to(block[None], (len(groups[0]),) + block.shape)
    return lax.all_to_all(copies, axes, 0, 0, axis_index_groups=groups)


def columns():
    def at(x, y, z, c):
        return (((x * 4 + z // 4) * 4 + y) * 4 + z % 4) * 2 + c

    return [[at(k, j, z, 0) for j in range(4) for z in range(16)] for k in range(4)] + [
        [at(j, k, z, 1) for j in range(4) for z in range(16)] for k in range(4)
    ]


def lines():
    return [[(i * 4 + k) * 2 for i in range(4)] for k in range(4)] + [
        [(k * 4 + i) * 2 + 1 for i in range(4)] for k in range(4)
    ]


def product(rows_ref, w_ref):
    return lax.dot_general(rows_ref[...], w_ref[...], (((1,), (1,)), ((), ())), preferred_element_type=F32)


def first_kernel(rows_ref, w_ref, out_ref):
    out_ref[...] = product(rows_ref, w_ref)


def encode(partial):
    rows, width = partial.shape
    top = jnp.max(jnp.abs(partial), axis=1, keepdims=True)
    power = jnp.clip(jnp.floor(jnp.log2(top)), -80.0, 80.0)
    mantissa = jnp.ceil(top * jnp.exp2(-power) * 8192.0) + 1.0
    step = mantissa * jnp.exp2(power) * (1.0 / (8192.0 * TOP))
    codes = jnp.clip(jnp.round(partial * (1.0 / step)), -TOP, TOP)
    codes = jnp.concatenate([codes, jnp.zeros((rows, LANES - width), F32)], axis=1)
    column = lax.broadcasted_iota(I32, (rows, LANES), 1)
    codes = jnp.where(column == width, mantissa, codes)
    codes = jnp.where(column == width + 1, power, codes)
    high = jnp.floor(codes * (1.0 / 256.0))
    return high.astype(BF16), (codes - high * 256.0).astype(BF16)


def second_kernel(rows_ref, w_ref, first_ref, place_ref, out_ref, high_ref, low_ref):
    half = first_ref.shape[0]
    high_ref[:half], low_ref[:half] = encode(first_ref[...])
    high_ref[half:], low_ref[half:] = encode(product(rows_ref, w_ref))
    for at in range(0, 512, 256):
        column = lax.broadcasted_iota(I32, (256, 512), 1)
        pick = jnp.where(place_ref[at : at + 256] == column, 1.0, 0.0).astype(BF16)
        high = jnp.dot(pick, high_ref[...], preferred_element_type=F32)
        low = jnp.dot(pick, low_ref[...], preferred_element_type=F32)
        out_ref[at : at + 256] = (high * 256.0 + low).astype(I32).astype(I16)


def decode_kernel(coefficient_ref, got_ref, out_ref):
    rows, cands, width = out_ref.shape
    totals = [None] * cands
    for source in range(16):
        codes = got_ref[source * rows : (source + 1) * rows].astype(I32).astype(F32)
        step = codes[:, width : width + 1] * jnp.exp2(codes[:, width + 1 : width + 2]) * (1.0 / (8192.0 * TOP))
        values = codes * step
        for c in range(cands):
            term = coefficient_ref[c, source] * values
            totals[c] = term if source == 0 else totals[c] + term
    out_ref[...] = jnp.stack([t[:, :width] for t in totals], axis=1).astype(BF16)


def on_device(weights, calib_pool, cand_index, coef_table, row_ids):
    core = lax.axis_index("c")
    w_piece = weights[0].T
    own = spread(calib_pool.reshape(32, 128), AXES, columns()).reshape(64, 4096)
    own = spread(own, ("x", "y", "c"), lines()).reshape(256, 4096)
    other = lax.ppermute(own, "c", [(0, 1), (1, 0)])

    width = w_piece.shape[0]
    vmem = pl.BlockSpec(memory_space=pltpu.VMEM)
    params = pltpu.CompilerParams(vmem_limit_bytes=40 * 2**20)
    cost = pl.CostEstimate(flops=2 * 256 * 4096 * width, bytes_accessed=6 * 2**20, transcendentals=0)
    first = pl.pallas_call(
        first_kernel,
        out_shape=jax.ShapeDtypeStruct((256, width), F32),
        in_specs=[vmem] * 2,
        out_specs=vmem,
        compiler_params=params,
        cost_estimate=cost,
        name="first",
    )(own, w_piece)

    x, zh, y, zl, c = (row_ids >> 7) & 3, (row_ids >> 5) & 3, (row_ids >> 3) & 3, (row_ids >> 1) & 3, row_ids & 1
    place = jnp.where(c == 0, x * 4 + y, y * 4 + x) * 16 + zh * 4 + zl + jnp.where(c == core, 0, 256)

    sent = pl.pallas_call(
        second_kernel,
        out_shape=jax.ShapeDtypeStruct((512, LANES), I16),
        in_specs=[vmem] * 4,
        out_specs=vmem,
        scratch_shapes=[pltpu.VMEM((512, LANES), BF16)] * 2,
        compiler_params=params,
        cost_estimate=cost,
        name="second",
    )(other, w_piece, first, place[:, None])
    got = lax.all_to_all(sent, ("x", "zh"), 0, 0, tiled=True)

    entries = jnp.arange(coef_table.shape[0], dtype=I32)
    onehot = (cand_index[:, :, None] == entries[None, None, :]).astype(F32)
    coefficient = jnp.sum(onehot * coef_table[None, None, :], axis=2)
    return pl.pallas_call(
        decode_kernel,
        out_shape=jax.ShapeDtypeStruct((32, 4, width), BF16),
        in_specs=[pl.BlockSpec(memory_space=pltpu.SMEM), vmem],
        out_specs=vmem,
        compiler_params=params,
        name="decode",
    )(coefficient, got)


def solution(mesh):
    fine = Mesh(mesh.devices.reshape(4, 4, 4, 4, 2), AXES)
    src, shard = ("x", "zh"), ("y", "zl", "c")
    placed = (P(src, None, shard), P(src + shard, None), P(), P(), P())
    return jax.shard_map(on_device, mesh=fine, in_specs=placed, out_specs=P(src, None, shard), check_vma=False)
```

```python
import jax
import jax.numpy as jnp
from jax import lax
from jax.experimental import pallas as pl
from jax.experimental.pallas import tpu as pltpu
from jax.sharding import Mesh, PartitionSpec as P

BF16, F32, I16, I32 = jnp.bfloat16, jnp.float32, jnp.int16, jnp.int32
LANES = 512
TOP = 32767.0
AXES = ("x", "zh", "y", "zl", "c")


def spread(block, axes, count, groups=None):
    copies = jnp.broadcast_to(block[None], (count,) + block.shape)
    return lax.all_to_all(copies, axes, 0, 0, axis_index_groups=groups)


def lines(along):
    return [[(k * 4 + i) * 2 + along for i in range(4)] for k in range(4)] + [
        [(i * 4 + k) * 2 + 1 - along for i in range(4)] for k in range(4)
    ]


def product(rows_ref, w_ref):
    return lax.dot_general(rows_ref[...], w_ref[...], (((1,), (1,)), ((), ())), preferred_element_type=F32)


def first_kernel(rows_ref, w_ref, out_ref):
    out_ref[...] = product(rows_ref, w_ref)


def encode(partial, out_ref, at):
    rows, width = partial.shape
    main = LANES - 128
    top = jnp.max(jnp.abs(partial), axis=1, keepdims=True)
    power = jnp.clip(jnp.floor(jnp.log2(top)), -80.0, 80.0)
    mantissa = jnp.ceil(top * jnp.exp2(-power) * 8192.0) + 1.0
    per_step = 1.0 / (mantissa * jnp.exp2(power) * (1.0 / (8192.0 * TOP)))
    tail = jnp.concatenate([partial[:, main:], jnp.zeros((rows, LANES - width), F32)], axis=1)
    tail = jnp.round(tail * per_step)
    column = lax.broadcasted_iota(I32, (rows, 128), 1) + main
    tail = jnp.where(column == width, mantissa, jnp.where(column == width + 1, power, tail))
    for codes, columns in ((jnp.round(partial[:, :main] * per_step), slice(0, main)), (tail, slice(main, LANES))):
        high = jnp.floor(codes * (1.0 / 256.0))
        out_ref[at : at + rows, columns] = high.astype(BF16)
        out_ref[512 + at : 512 + at + rows, columns] = (codes - high * 256.0).astype(BF16)


def second_kernel(rows_ref, w_ref, first_ref, place_ref, out_ref, bytes_ref):
    half = first_ref.shape[0]
    encode(first_ref[...], bytes_ref, 0)
    encode(product(rows_ref, w_ref), bytes_ref, half)
    for at in range(0, 512, 256):
        column = lax.broadcasted_iota(I32, (256, 512), 1)
        found = place_ref[at : at + 256] == column
        pick = jnp.concatenate([jnp.where(found, 256.0, 0.0), jnp.where(found, 1.0, 0.0)], axis=1).astype(BF16)
        codes = jnp.dot(pick, bytes_ref[...], preferred_element_type=F32)
        out_ref[at : at + 256] = codes.astype(I32).astype(I16)


def decode_kernel(coefficient_ref, got_ref, out_ref):
    rows, cands, width = out_ref.shape
    totals = [None] * cands
    for source in range(16):
        codes = got_ref[source * rows : (source + 1) * rows].astype(I32).astype(F32)
        step = codes[:, width : width + 1] * jnp.exp2(codes[:, width + 1 : width + 2]) * (1.0 / (8192.0 * TOP))
        values = codes * step
        for c in range(cands):
            term = coefficient_ref[c, source] * values
            totals[c] = term if source == 0 else totals[c] + term
    out_ref[...] = jnp.stack([t[:, :width] for t in totals], axis=1).astype(BF16)


def on_device(weights, calib_pool, cand_index, coef_table, row_ids):
    core = lax.axis_index("c")
    w_piece = weights[0].T
    own = spread(calib_pool.reshape(32, 128), ("zh", "zl"), 16).reshape(16, 4096)
    own = spread(own, ("x", "y", "c"), 4, lines(0)).reshape(64, 4096)
    own = spread(own, ("x", "y", "c"), 4, lines(1)).reshape(256, 4096)
    other = lax.ppermute(own, "c", [(0, 1), (1, 0)])

    width = w_piece.shape[0]
    vmem = pl.BlockSpec(memory_space=pltpu.VMEM)
    params = pltpu.CompilerParams(vmem_limit_bytes=16 * 2**20)
    cost = pl.CostEstimate(flops=2 * 256 * 4096 * width, bytes_accessed=6 * 2**20, transcendentals=0)
    first = pl.pallas_call(
        first_kernel,
        out_shape=jax.ShapeDtypeStruct((256, width), F32),
        in_specs=[vmem] * 2,
        out_specs=vmem,
        compiler_params=params,
        cost_estimate=cost,
        name="first",
    )(own, w_piece)

    x, zh, y, zl, c = (row_ids >> 7) & 3, (row_ids >> 5) & 3, (row_ids >> 3) & 3, (row_ids >> 1) & 3, row_ids & 1
    place = jnp.where(c == 0, x * 4 + y, y * 4 + x) * 16 + zh * 4 + zl + jnp.where(c == core, 0, 256)

    sent = pl.pallas_call(
        second_kernel,
        out_shape=jax.ShapeDtypeStruct((512, LANES), I16),
        in_specs=[vmem] * 4,
        out_specs=vmem,
        scratch_shapes=[pltpu.VMEM((1024, LANES), BF16)],
        compiler_params=params,
        cost_estimate=cost,
        name="second",
    )(other, w_piece, first, place[:, None])
    got = lax.all_to_all(sent, ("x", "zh"), 0, 0, tiled=True)

    entries = jnp.arange(coef_table.shape[0], dtype=I32)
    onehot = (cand_index[:, :, None] == entries[None, None, :]).astype(F32)
    coefficient = jnp.sum(onehot * coef_table[None, None, :], axis=2)
    return pl.pallas_call(
        decode_kernel,
        out_shape=jax.ShapeDtypeStruct((32, 4, width), BF16),
        in_specs=[pl.BlockSpec(memory_space=pltpu.SMEM), vmem],
        out_specs=vmem,
        compiler_params=params,
        name="decode",
    )(coefficient, got)


def solution(mesh):
    fine = Mesh(mesh.devices.reshape(4, 4, 4, 4, 2), AXES)
    src, shard = ("x", "zh"), ("y", "zl", "c")
    placed = (P(src, None, shard), P(src + shard, None), P(), P(), P())
    return jax.shard_map(on_device, mesh=fine, in_specs=placed, out_specs=P(src, None, shard), check_vma=False)
```

```python
import jax
import jax.numpy as jnp
from jax import lax
from jax.experimental import pallas as pl
from jax.experimental.pallas import tpu as pltpu
from jax.sharding import Mesh, PartitionSpec as P

BF16, F32, I16, I32 = jnp.bfloat16, jnp.float32, jnp.int16, jnp.int32
LANES = 512
TOP = 32767.0
AXES = ("x", "zh", "y", "zl", "c")


def spread(block, axes, count, groups=None):
    copies = jnp.broadcast_to(block[None], (count,) + block.shape)
    return lax.all_to_all(copies, axes, 0, 0, axis_index_groups=groups)


def lines(along):
    return [[(k * 4 + i) * 2 + along for i in range(4)] for k in range(4)] + [
        [(i * 4 + k) * 2 + 1 - along for i in range(4)] for k in range(4)
    ]


def encode(partial, out_ref):
    rows, width = partial.shape
    main = LANES - 128
    top = jnp.max(jnp.abs(partial), axis=1, keepdims=True)
    power = jnp.clip(jnp.floor(jnp.log2(top)), -80.0, 80.0)
    mantissa = jnp.ceil(top * jnp.exp2(-power) * 8192.0) + 1.0
    per_step = 1.0 / (mantissa * jnp.exp2(power) * (1.0 / (8192.0 * TOP)))
    tail = jnp.concatenate([partial[:, main:], jnp.zeros((rows, LANES - width), F32)], axis=1)
    tail = jnp.round(tail * per_step)
    column = lax.broadcasted_iota(I32, (rows, 128), 1) + main
    tail = jnp.where(column == width, mantissa, jnp.where(column == width + 1, power, tail))
    for codes, columns in ((jnp.round(partial[:, :main] * per_step), slice(0, main)), (tail, slice(main, LANES))):
        high = jnp.floor(codes * (1.0 / 256.0))
        out_ref[:rows, columns] = high.astype(BF16)
        out_ref[rows:, columns] = (codes - high * 256.0).astype(BF16)


def coded_kernel(rows_ref, w_ref, out_ref):
    encode(lax.dot_general(rows_ref[...], w_ref[...], (((1,), (1,)), ((), ())), preferred_element_type=F32), out_ref)


def pick_kernel(place_ref, own_ref, other_ref, out_ref):
    column = lax.broadcasted_iota(I32, (256, 256), 1)
    lane16, lane8 = lax.broadcasted_iota(I32, (16, 128), 1), lax.broadcasted_iota(I32, (8, 128), 1)
    for at in range(0, 512, 256):
        place = place_ref[at : at + 256]
        picks = []
        for half in (0, 256):
            found = place - half == column
            picks += [jnp.where(found, 256.0, 0.0).astype(BF16), jnp.where(found, 1.0, 0.0).astype(BF16)]
        codes = jnp.dot(jnp.concatenate(picks[:2], axis=1), own_ref[...], preferred_element_type=F32)
        codes += jnp.dot(jnp.concatenate(picks[2:], axis=1), other_ref[...], preferred_element_type=F32)
        for block in range(8):
            owner = at // 32 + block
            to = owner % 4 * 4 + owner // 4
            rows = codes[block * 32 : block * 32 + 32]
            tail = rows[:, 384:]
            fold = jnp.where(lane16 < 64, tail[:16], pltpu.roll(tail[16:], 64, 1))
            a, b, c, d = (pltpu.roll(tail[8 * i : 8 * i + 8], (64 + 32 * i) % 128, 1) for i in range(4))
            last = jnp.where(lane8 < 64, jnp.where(lane8 < 32, a, b), jnp.where(lane8 < 96, c, d))
            packed = jnp.concatenate([rows[:, :128], rows[:, 128:256], rows[:, 256:384], fold, last], axis=0)
            out_ref[to] = packed.astype(I32).astype(I16)


def decode_kernel(coefficient_ref, got_ref, out_ref):
    rows, cands, width = out_ref.shape
    lane = lax.broadcasted_iota(I32, (32, 128), 1)
    totals = [None] * cands
    for source in range(16):
        codes = got_ref[source].astype(I32).astype(F32)
        fold, last = codes[96:112], codes[112:120]
        folds = jnp.concatenate([fold, pltpu.roll(fold, 64, 1)], axis=0)
        lasts = jnp.concatenate([pltpu.roll(last, (64 - 32 * i) % 128, 1) for i in range(4)], axis=0)
        tail = jnp.where(lane < 64, folds, lasts)
        at = width % 128
        step = tail[:, at : at + 1] * jnp.exp2(tail[:, at + 1 : at + 2]) * (1.0 / (8192.0 * TOP))
        values = jnp.concatenate([codes[:32], codes[32:64], codes[64:96], tail], axis=1) * step
        for c in range(cands):
            term = coefficient_ref[c, source % 4 * 4 + source // 4] * values
            totals[c] = term if source == 0 else totals[c] + term
    out_ref[...] = jnp.stack([t[:, :width] for t in totals], axis=1).astype(BF16)


def on_device(weights, calib_pool, cand_index, coef_table, row_ids):
    core = lax.axis_index("c")
    swap = [(0, 1), (1, 0)]
    w_piece = weights[0].T
    own = spread(calib_pool.reshape(32, 128), ("zh", "zl"), 16).reshape(16, 4096)
    own = spread(own, ("x", "y", "c"), 4, lines(0)).reshape(64, 4096)
    own, w_mine = lax.optimization_barrier((own, w_piece))
    w_other = lax.ppermute(w_mine, "c", swap)
    own = spread(own, ("x", "y", "c"), 4, lines(1)).reshape(256, 4096)

    width = w_piece.shape[0]
    vmem = pl.BlockSpec(memory_space=pltpu.VMEM)
    params = pltpu.CompilerParams(vmem_limit_bytes=16 * 2**20)

    def coded(w):
        return pl.pallas_call(
            coded_kernel,
            out_shape=jax.ShapeDtypeStruct((512, LANES), BF16),
            in_specs=[vmem] * 2,
            out_specs=vmem,
            compiler_params=params,
            cost_estimate=pl.CostEstimate(flops=2 * 256 * 4096 * width, bytes_accessed=6 * 2**20, transcendentals=0),
            name="coded",
        )(own, w)

    from_other = lax.ppermute(coded(w_other), "c", swap)
    mine = coded(w_piece)

    x, zh, y, zl, c = (row_ids >> 7) & 3, (row_ids >> 5) & 3, (row_ids >> 3) & 3, (row_ids >> 1) & 3, row_ids & 1
    place = jnp.where(c == 0, x * 4 + y, y * 4 + x) * 16 + zh * 4 + zl + jnp.where(c == core, 0, 256)
    sent = pl.pallas_call(
        pick_kernel,
        out_shape=jax.ShapeDtypeStruct((16, 120, 128), I16),
        in_specs=[vmem] * 3,
        out_specs=vmem,
        compiler_params=params,
        cost_estimate=pl.CostEstimate(flops=2**29, bytes_accessed=2**21, transcendentals=0),
        name="pick",
    )(place[:, None], mine, from_other)
    got = lax.all_to_all(sent, ("zh", "x"), 0, 0)

    entries = jnp.arange(coef_table.shape[0], dtype=I32)
    onehot = (cand_index[:, :, None] == entries[None, None, :]).astype(F32)
    coefficient = jnp.sum(onehot * coef_table[None, None, :], axis=2)
    return pl.pallas_call(
        decode_kernel,
        out_shape=jax.ShapeDtypeStruct((32, 4, width), BF16),
        in_specs=[pl.BlockSpec(memory_space=pltpu.SMEM), vmem],
        out_specs=vmem,
        compiler_params=params,
        name="decode",
    )(coefficient, got)


def solution(mesh):
    fine = Mesh(mesh.devices.reshape(4, 4, 4, 4, 2), AXES)
    src, shard = ("x", "zh"), ("y", "zl", "c")
    placed = (P(src, None, shard), P(src + shard, None), P(), P(), P())
    return jax.shard_map(on_device, mesh=fine, in_specs=placed, out_specs=P(src, None, shard), check_vma=False)
```

```python
import jax
import jax.numpy as jnp
from jax import lax
from jax.experimental import pallas as pl
from jax.experimental.pallas import tpu as pltpu
from jax.sharding import Mesh, PartitionSpec as P

BF16, F32, I16, I32 = jnp.bfloat16, jnp.float32, jnp.int16, jnp.int32
LANES = 512
TOP = 32767.0
AXES = ("x", "zh", "y", "zl", "c")


def spread(block, axes, count, groups=None):
    copies = jnp.broadcast_to(block[None], (count,) + block.shape)
    return lax.all_to_all(copies, axes, 0, 0, axis_index_groups=groups)


def lines(along):
    return [[(k * 4 + i) * 2 + along for i in range(4)] for k in range(4)] + [
        [(i * 4 + k) * 2 + 1 - along for i in range(4)] for k in range(4)
    ]


def encode(partial, out_ref):
    rows, width = partial.shape
    main = LANES - 128
    top = jnp.max(jnp.abs(partial), axis=1, keepdims=True)
    power = jnp.clip(jnp.floor(jnp.log2(top)), -80.0, 80.0)
    mantissa = jnp.ceil(top * jnp.exp2(-power) * 8192.0) + 1.0
    per_step = 1.0 / (mantissa * jnp.exp2(power) * (1.0 / (8192.0 * TOP)))
    tail = jnp.concatenate([partial[:, main:], jnp.zeros((rows, LANES - width), F32)], axis=1)
    tail = jnp.round(tail * per_step)
    column = lax.broadcasted_iota(I32, (rows, 128), 1) + main
    tail = jnp.where(column == width, mantissa, jnp.where(column == width + 1, power, tail))
    for codes, columns in ((jnp.round(partial[:, :main] * per_step), slice(0, main)), (tail, slice(main, LANES))):
        high = jnp.floor(codes * (1.0 / 256.0))
        out_ref[:rows, columns] = high.astype(BF16)
        out_ref[rows:, columns] = (codes - high * 256.0).astype(BF16)


def coded_kernel(rows_ref, w_ref, out_ref):
    encode(lax.dot_general(rows_ref[...], w_ref[...], (((1,), (1,)), ((), ())), preferred_element_type=F32), out_ref)


def streamed_kernel(rows_ref, w_ref, out_ref, w_here, arrived):
    pieces, _, depth = w_here.shape
    copies = [
        pltpu.make_async_copy(w_ref.at[:, pl.ds(k * depth, depth)], w_here.at[k], arrived.at[k]) for k in range(pieces)
    ]
    for copy in copies:
        copy.start()
    total = None
    for k, copy in enumerate(copies):
        copy.wait()
        term = lax.dot_general(
            rows_ref[:, k * depth : (k + 1) * depth], w_here[k], (((1,), (1,)), ((), ())), preferred_element_type=F32
        )
        total = term if k == 0 else total + term
    encode(total, out_ref)


def pick_kernel(place_ref, own_ref, other_ref, out_ref):
    column = lax.broadcasted_iota(I32, (256, 256), 1)
    lane16, lane8 = lax.broadcasted_iota(I32, (16, 128), 1), lax.broadcasted_iota(I32, (8, 128), 1)
    for at in range(0, 512, 256):
        place = place_ref[at : at + 256]
        picks = []
        for half in (0, 256):
            found = place - half == column
            picks += [jnp.where(found, 256.0, 0.0).astype(BF16), jnp.where(found, 1.0, 0.0).astype(BF16)]
        codes = jnp.dot(jnp.concatenate(picks[:2], axis=1), own_ref[...], preferred_element_type=F32)
        codes += jnp.dot(jnp.concatenate(picks[2:], axis=1), other_ref[...], preferred_element_type=F32)
        for block in range(8):
            owner = at // 32 + block
            to = owner % 4 * 4 + owner // 4
            rows = codes[block * 32 : block * 32 + 32]
            tail = rows[:, 384:]
            fold = jnp.where(lane16 < 64, tail[:16], pltpu.roll(tail[16:], 64, 1))
            a, b, c, d = (pltpu.roll(tail[8 * i : 8 * i + 8], (64 + 32 * i) % 128, 1) for i in range(4))
            last = jnp.where(lane8 < 64, jnp.where(lane8 < 32, a, b), jnp.where(lane8 < 96, c, d))
            packed = jnp.concatenate([rows[:, :128], rows[:, 128:256], rows[:, 256:384], fold, last], axis=0)
            out_ref[to] = packed.astype(I32).astype(I16)


def decode_kernel(coefficient_ref, got_ref, out_ref, tail_ref, step_ref):
    rows, cands, width = out_ref.shape
    lane = lax.broadcasted_iota(I32, (rows, 128), 1)
    at = width % 128
    for source in range(16):
        codes = got_ref[source, 96:].astype(I32).astype(F32)
        fold, last = codes[:16], codes[16:]
        folds = jnp.concatenate([fold, pltpu.roll(fold, 64, 1)], axis=0)
        lasts = jnp.concatenate([pltpu.roll(last, (64 - 32 * i) % 128, 1) for i in range(4)], axis=0)
        tail = jnp.where(lane < 64, folds, lasts)
        step = tail[:, at : at + 1] * jnp.exp2(tail[:, at + 1 : at + 2]) * (1.0 / (8192.0 * TOP))
        tail_ref[source] = tail * step
        step_ref[source] = jnp.broadcast_to(step, (rows, 128))
    for block in range(4):
        totals = [None] * cands
        for source in range(16):
            if block < 3:
                codes = got_ref[source, 32 * block : 32 * block + 32].astype(I32).astype(F32)
                values = codes * step_ref[source]
            else:
                values = tail_ref[source]
            for c in range(cands):
                term = coefficient_ref[c, source % 4 * 4 + source // 4] * values
                totals[c] = term if source == 0 else totals[c] + term
        columns = slice(128 * block, min(128 * block + 128, width))
        stacked = jnp.stack([t[:, : columns.stop - columns.start] for t in totals], axis=1)
        out_ref[:, :, columns] = stacked.astype(BF16)


def on_device(weights, calib_pool, cand_index, coef_table, row_ids):
    core = lax.axis_index("c")
    swap = [(0, 1), (1, 0)]
    w_piece = weights[0].T
    own = spread(calib_pool.reshape(32, 128), ("zh", "zl"), 16).reshape(16, 4096)
    own = spread(own, ("x", "y", "c"), 4, lines(0)).reshape(64, 4096)
    own, w_mine = lax.optimization_barrier((own, w_piece))
    w_other = lax.ppermute(w_mine, "c", swap)
    own = spread(own, ("x", "y", "c"), 4, lines(1)).reshape(256, 4096)

    width = w_piece.shape[0]
    vmem = pl.BlockSpec(memory_space=pltpu.VMEM)
    params = pltpu.CompilerParams(vmem_limit_bytes=16 * 2**20)

    def coded(kernel, w, w_spec, scratch):
        return pl.pallas_call(
            kernel,
            out_shape=jax.ShapeDtypeStruct((512, LANES), BF16),
            in_specs=[vmem, w_spec],
            out_specs=vmem,
            scratch_shapes=scratch,
            compiler_params=params,
            cost_estimate=pl.CostEstimate(flops=2 * 256 * 4096 * width, bytes_accessed=6 * 2**20, transcendentals=0),
            name="coded",
        )(own, w)

    from_other = lax.ppermute(coded(coded_kernel, w_other, vmem, []), "c", swap)
    pieces = [pltpu.VMEM((4, width, 1024), BF16), pltpu.SemaphoreType.DMA((4,))]
    here = pltpu.with_memory_space_constraint(w_piece, pltpu.HBM)
    mine = coded(streamed_kernel, here, pl.BlockSpec(memory_space=pltpu.HBM), pieces)

    x, zh, y, zl, c = (row_ids >> 7) & 3, (row_ids >> 5) & 3, (row_ids >> 3) & 3, (row_ids >> 1) & 3, row_ids & 1
    place = jnp.where(c == 0, x * 4 + y, y * 4 + x) * 16 + zh * 4 + zl + jnp.where(c == core, 0, 256)
    sent = pl.pallas_call(
        pick_kernel,
        out_shape=jax.ShapeDtypeStruct((16, 120, 128), I16),
        in_specs=[vmem] * 3,
        out_specs=vmem,
        compiler_params=params,
        cost_estimate=pl.CostEstimate(flops=2**29, bytes_accessed=2**21, transcendentals=0),
        name="pick",
    )(place[:, None], mine, from_other)
    got = lax.all_to_all(sent, ("zh", "x"), 0, 0)

    entries = jnp.arange(coef_table.shape[0], dtype=I32)
    onehot = (cand_index[:, :, None] == entries[None, None, :]).astype(F32)
    coefficient = jnp.sum(onehot * coef_table[None, None, :], axis=2)
    return pl.pallas_call(
        decode_kernel,
        out_shape=jax.ShapeDtypeStruct((32, 4, width), BF16),
        in_specs=[pl.BlockSpec(memory_space=pltpu.SMEM), vmem],
        out_specs=vmem,
        compiler_params=params,
        scratch_shapes=[pltpu.VMEM((16, 32, 128), F32)] * 2,
        name="decode",
    )(coefficient, got)


def solution(mesh):
    fine = Mesh(mesh.devices.reshape(4, 4, 4, 4, 2), AXES)
    src, shard = ("x", "zh"), ("y", "zl", "c")
    placed = (P(src, None, shard), P(src + shard, None), P(), P(), P())
    return jax.shard_map(on_device, mesh=fine, in_specs=placed, out_specs=P(src, None, shard), check_vma=False)
```

```python
import jax
import jax.numpy as jnp
from jax import lax
from jax.experimental import pallas as pl
from jax.experimental.pallas import tpu as pltpu
from jax.sharding import Mesh, PartitionSpec as P

BF16, F32, I16, I32 = jnp.bfloat16, jnp.float32, jnp.int16, jnp.int32
LANES = 512
TOP = 32767.0
AXES = ("x", "zh", "y", "zl", "c")


def spread(block, axes):
    return lax.all_to_all(jnp.broadcast_to(block[None], (16,) + block.shape), axes, 0, 0)


def encode(partial, out_ref):
    rows, width = partial.shape
    main = LANES - 128
    top = jnp.max(jnp.abs(partial), axis=1, keepdims=True)
    power = jnp.clip(jnp.floor(jnp.log2(top)), -80.0, 80.0)
    mantissa = jnp.ceil(top * jnp.exp2(-power) * 8192.0) + 1.0
    per_step = 1.0 / (mantissa * jnp.exp2(power) * (1.0 / (8192.0 * TOP)))
    tail = jnp.concatenate([partial[:, main:], jnp.zeros((rows, LANES - width), F32)], axis=1)
    tail = jnp.round(tail * per_step)
    column = lax.broadcasted_iota(I32, (rows, 128), 1) + main
    tail = jnp.where(column == width, mantissa, jnp.where(column == width + 1, power, tail))
    for codes, columns in ((jnp.round(partial[:, :main] * per_step), slice(0, main)), (tail, slice(main, LANES))):
        high = jnp.floor(codes * (1.0 / 256.0))
        out_ref[:rows, columns] = high.astype(BF16)
        out_ref[rows:, columns] = (codes - high * 256.0).astype(BF16)


def times(rows, weights):
    return lax.dot_general(rows, weights, (((1,), (1,)), ((), ())), preferred_element_type=F32)


def picked(place, half, bytes_ref):
    found = place - half == lax.broadcasted_iota(I32, (place.shape[0], 256), 1)
    pick = jnp.concatenate([jnp.where(found, 256.0, 0.0), jnp.where(found, 1.0, 0.0)], axis=1).astype(BF16)
    return jnp.dot(pick, bytes_ref[...], preferred_element_type=F32)


def product(rows_ref, w_ref, far_ref, near_ref, arrived):
    pieces = arrived.shape[0]
    depth = far_ref.shape[1] // pieces
    copies = []
    for k in range(pieces):
        part = pl.ds(k * depth, depth)
        copies.append(pltpu.make_async_copy(far_ref.at[:, part], near_ref.at[:, part], arrived.at[k]))
        copies[k].start()
    total = None
    for k, copy in enumerate(copies):
        copy.wait()
        part = slice(k * depth, (k + 1) * depth)
        term = times(rows_ref[:, part], w_ref[:, part])
        total = term if k == 0 else total + term
    return total


def own_kernel(place_ref, rows_ref, far_ref, out_ref, w_ref, bytes_ref, arrived):
    encode(product(rows_ref, w_ref, far_ref, w_ref, arrived), bytes_ref)
    out_ref[...] = picked(place_ref[...], 0, bytes_ref)


def other_kernel(place_ref, far_ref, w_ref, own_ref, out_ref, rows_ref, bytes_ref, arrived):
    encode(product(rows_ref, w_ref, far_ref, rows_ref, arrived), bytes_ref)
    lane16, lane8 = lax.broadcasted_iota(I32, (16, 128), 1), lax.broadcasted_iota(I32, (8, 128), 1)
    for at in range(0, 512, 256):
        codes = own_ref[at : at + 256] + picked(place_ref[at : at + 256], 256, bytes_ref)
        for block in range(8):
            owner = at // 32 + block
            to = owner % 4 * 4 + owner // 4
            rows = codes[block * 32 : block * 32 + 32]
            tail = rows[:, 384:]
            fold = jnp.where(lane16 < 64, tail[:16], pltpu.roll(tail[16:], 64, 1))
            a, b, c, d = (pltpu.roll(tail[8 * i : 8 * i + 8], (64 + 32 * i) % 128, 1) for i in range(4))
            last = jnp.where(lane8 < 64, jnp.where(lane8 < 32, a, b), jnp.where(lane8 < 96, c, d))
            packed = jnp.concatenate([rows[:, :128], rows[:, 128:256], rows[:, 256:384], fold, last], axis=0)
            out_ref[to] = packed.astype(I32).astype(I16)


def decode_kernel(coefficient_ref, got_ref, out_ref, tail_ref, step_ref):
    rows, cands, width = out_ref.shape
    lane = lax.broadcasted_iota(I32, (rows, 128), 1)
    at = width % 128
    for source in range(16):
        codes = got_ref[source, 96:].astype(I32).astype(F32)
        fold, last = codes[:16], codes[16:]
        folds = jnp.concatenate([fold, pltpu.roll(fold, 64, 1)], axis=0)
        lasts = jnp.concatenate([pltpu.roll(last, (64 - 32 * i) % 128, 1) for i in range(4)], axis=0)
        tail = jnp.where(lane < 64, folds, lasts)
        step = tail[:, at : at + 1] * jnp.exp2(tail[:, at + 1 : at + 2]) * (1.0 / (8192.0 * TOP))
        tail_ref[source] = tail * step
        step_ref[source] = jnp.broadcast_to(step, (rows, 128))
    for block in range(4):
        totals = [None] * cands
        for source in range(16):
            if block < 3:
                codes = got_ref[source, 32 * block : 32 * block + 32].astype(I32).astype(F32)
                values = codes * step_ref[source]
            else:
                values = tail_ref[source]
            for c in range(cands):
                term = coefficient_ref[c, source % 4 * 4 + source // 4] * values
                totals[c] = term if source == 0 else totals[c] + term
        columns = slice(128 * block, min(128 * block + 128, width))
        stacked = jnp.stack([t[:, : columns.stop - columns.start] for t in totals], axis=1)
        out_ref[:, :, columns] = stacked.astype(BF16)


def on_device(weights, calib_pool, cand_index, coef_table, row_ids):
    core = lax.axis_index("c")
    w_piece = weights[0].T
    own = spread(calib_pool.reshape(32, 128), ("zh", "zl")).reshape(16, 4096)
    own = spread(own, ("x", "y")).reshape(256, 4096)
    other = lax.ppermute(own, "c", [(0, 1), (1, 0)])

    x, zh, y, zl, c = (row_ids >> 7) & 3, (row_ids >> 5) & 3, (row_ids >> 3) & 3, (row_ids >> 1) & 3, row_ids & 1
    place = (((x * 4 + y) * 4 + zh) * 4 + zl + jnp.where(c == core, 0, 256))[:, None]

    width = w_piece.shape[0]
    vmem, far = pl.BlockSpec(memory_space=pltpu.VMEM), pl.BlockSpec(memory_space=pltpu.HBM)
    params = pltpu.CompilerParams(vmem_limit_bytes=16 * 2**20)
    cost = pl.CostEstimate(flops=2 * 256 * 4096 * width, bytes_accessed=6 * 2**20, transcendentals=0)
    codes, w_here = pl.pallas_call(
        own_kernel,
        out_shape=(jax.ShapeDtypeStruct((512, LANES), F32), jax.ShapeDtypeStruct(w_piece.shape, BF16)),
        in_specs=[vmem, vmem, far],
        out_specs=(vmem, vmem),
        scratch_shapes=[pltpu.VMEM((512, LANES), BF16), pltpu.SemaphoreType.DMA((4,))],
        compiler_params=params,
        cost_estimate=cost,
        name="own",
    )(place, own, pltpu.with_memory_space_constraint(w_piece, pltpu.HBM))
    sent = pl.pallas_call(
        other_kernel,
        out_shape=jax.ShapeDtypeStruct((16, 120, 128), I16),
        in_specs=[vmem, far, vmem, vmem],
        out_specs=vmem,
        scratch_shapes=[pltpu.VMEM((256, 4096), BF16), pltpu.VMEM((512, LANES), BF16), pltpu.SemaphoreType.DMA((4,))],
        compiler_params=params,
        cost_estimate=cost,
        name="other",
    )(place, pltpu.with_memory_space_constraint(other, pltpu.HBM), w_here, codes)
    got = lax.all_to_all(sent, ("zh", "x"), 0, 0)

    entries = jnp.arange(coef_table.shape[0], dtype=I32)
    onehot = (cand_index[:, :, None] == entries[None, None, :]).astype(F32)
    coefficient = jnp.sum(onehot * coef_table[None, None, :], axis=2)
    return pl.pallas_call(
        decode_kernel,
        out_shape=jax.ShapeDtypeStruct((32, 4, width), BF16),
        in_specs=[pl.BlockSpec(memory_space=pltpu.SMEM), vmem],
        out_specs=vmem,
        compiler_params=params,
        scratch_shapes=[pltpu.VMEM((16, 32, 128), F32)] * 2,
        name="decode",
    )(coefficient, got)


def solution(mesh):
    fine = Mesh(mesh.devices.reshape(4, 4, 4, 4, 2), AXES)
    src, shard = ("x", "zh"), ("y", "zl", "c")
    placed = (P(src, None, shard), P(src + shard, None), P(), P(), P())
    return jax.shard_map(on_device, mesh=fine, in_specs=placed, out_specs=P(src, None, shard), check_vma=False)
```

```python
import jax
import jax.numpy as jnp
from jax import lax
from jax.experimental import pallas as pl
from jax.experimental.pallas import tpu as pltpu
from jax.sharding import Mesh, PartitionSpec as P

BF16, F32, I16, I32 = jnp.bfloat16, jnp.float32, jnp.int16, jnp.int32
LANES = 512
TOP = 32767.0
AXES = ("x", "zh", "y", "zl", "c")


def spread(block, axes):
    return lax.all_to_all(jnp.broadcast_to(block[None], (16,) + block.shape), axes, 0, 0)


def encode(partial, out_ref):
    rows, width = partial.shape
    main = LANES - 128
    top = jnp.max(jnp.abs(partial), axis=1, keepdims=True)
    power = jnp.clip(jnp.floor(jnp.log2(top)), -80.0, 80.0)
    mantissa = jnp.ceil(top * jnp.exp2(-power) * 8192.0) + 1.0
    per_step = 1.0 / (mantissa * jnp.exp2(power) * (1.0 / (8192.0 * TOP)))
    tail = jnp.concatenate([partial[:, main:], jnp.zeros((rows, LANES - width), F32)], axis=1)
    tail = jnp.round(tail * per_step)
    column = lax.broadcasted_iota(I32, (rows, 128), 1) + main
    tail = jnp.where(column == width, mantissa, jnp.where(column == width + 1, power, tail))
    for codes, columns in ((jnp.round(partial[:, :main] * per_step), slice(0, main)), (tail, slice(main, LANES))):
        high = jnp.floor(codes * (1.0 / 256.0))
        out_ref[:rows, columns] = high.astype(BF16)
        out_ref[rows:, columns] = (codes - high * 256.0).astype(BF16)


def coded_kernel(rows_ref, *refs):
    *w_refs, out_ref = refs
    parts = [
        lax.dot_general(rows_ref[...], w[...], (((1,), (1,)), ((), ())), preferred_element_type=F32) for w in w_refs
    ]
    encode(jnp.concatenate(parts, axis=1), out_ref)


def pick_kernel(place_ref, own_ref, other_ref, out_ref):
    column = lax.broadcasted_iota(I32, (256, 256), 1)
    lane16, lane8 = lax.broadcasted_iota(I32, (16, 128), 1), lax.broadcasted_iota(I32, (8, 128), 1)
    for at in range(0, 512, 256):
        place = place_ref[at : at + 256]
        picks = []
        for half in (0, 256):
            found = place - half == column
            picks += [jnp.where(found, 256.0, 0.0).astype(BF16), jnp.where(found, 1.0, 0.0).astype(BF16)]
        codes = jnp.dot(jnp.concatenate(picks[:2], axis=1), own_ref[...], preferred_element_type=F32)
        codes += jnp.dot(jnp.concatenate(picks[2:], axis=1), other_ref[...], preferred_element_type=F32)
        for block in range(8):
            owner = at // 32 + block
            to = owner % 4 * 4 + owner // 4
            rows = codes[block * 32 : block * 32 + 32]
            tail = rows[:, 384:]
            fold = jnp.where(lane16 < 64, tail[:16], pltpu.roll(tail[16:], 64, 1))
            a, b, c, d = (pltpu.roll(tail[8 * i : 8 * i + 8], (64 + 32 * i) % 128, 1) for i in range(4))
            last = jnp.where(lane8 < 64, jnp.where(lane8 < 32, a, b), jnp.where(lane8 < 96, c, d))
            packed = jnp.concatenate([rows[:, :128], rows[:, 128:256], rows[:, 256:384], fold, last], axis=0)
            out_ref[to] = packed.astype(I32).astype(I16)


def decode_kernel(coefficient_ref, got_ref, out_ref, tail_ref, step_ref):
    rows, cands, width = out_ref.shape
    lane = lax.broadcasted_iota(I32, (rows, 128), 1)
    at = width % 128
    for source in range(16):
        codes = got_ref[source, 96:].astype(I32).astype(F32)
        fold, last = codes[:16], codes[16:]
        folds = jnp.concatenate([fold, pltpu.roll(fold, 64, 1)], axis=0)
        lasts = jnp.concatenate([pltpu.roll(last, (64 - 32 * i) % 128, 1) for i in range(4)], axis=0)
        tail = jnp.where(lane < 64, folds, lasts)
        step = tail[:, at : at + 1] * jnp.exp2(tail[:, at + 1 : at + 2]) * (1.0 / (8192.0 * TOP))
        tail_ref[source] = tail * step
        step_ref[source] = jnp.broadcast_to(step, (rows, 128))
    for block in range(4):
        totals = [None] * cands
        for source in range(16):
            if block < 3:
                codes = got_ref[source, 32 * block : 32 * block + 32].astype(I32).astype(F32)
                values = codes * step_ref[source]
            else:
                values = tail_ref[source]
            for c in range(cands):
                term = coefficient_ref[c, source % 4 * 4 + source // 4] * values
                totals[c] = term if source == 0 else totals[c] + term
        columns = slice(128 * block, min(128 * block + 128, width))
        stacked = jnp.stack([t[:, : columns.stop - columns.start] for t in totals], axis=1)
        out_ref[:, :, columns] = stacked.astype(BF16)


def on_device(weights, calib_pool, cand_index, coef_table, row_ids):
    core = lax.axis_index("c")
    w_piece = weights[0].T
    swap = [(0, 1), (1, 0)]
    width = w_piece.shape[0]
    vmem = pl.BlockSpec(memory_space=pltpu.VMEM)
    params = pltpu.CompilerParams(vmem_limit_bytes=12 * 2**20)
    own = spread(calib_pool.reshape(32, 128), ("zh", "zl")).reshape(16, 4096)
    own, w_mine = lax.optimization_barrier((own, w_piece))
    w_other = [lax.ppermute(part, "c", swap) for part in (w_mine[:128], w_mine[128:256], w_mine[256:384], w_mine[384:])]
    own = spread(own, ("x", "y")).reshape(256, 4096)

    def coded(*w):
        return pl.pallas_call(
            coded_kernel,
            out_shape=jax.ShapeDtypeStruct((512, LANES), BF16),
            in_specs=[vmem] * (1 + len(w)),
            out_specs=vmem,
            compiler_params=params,
            cost_estimate=pl.CostEstimate(flops=2 * 256 * 4096 * width, bytes_accessed=6 * 2**20, transcendentals=0),
            name="coded",
        )(own, *w)

    from_other = lax.ppermute(coded(*w_other), "c", swap)
    mine = coded(w_piece)

    x, zh, y, zl, c = (row_ids >> 7) & 3, (row_ids >> 5) & 3, (row_ids >> 3) & 3, (row_ids >> 1) & 3, row_ids & 1
    place = ((x * 4 + y) * 4 + zh) * 4 + zl + jnp.where(c == core, 0, 256)
    sent = pl.pallas_call(
        pick_kernel,
        out_shape=jax.ShapeDtypeStruct((16, 120, 128), I16),
        in_specs=[vmem] * 3,
        out_specs=vmem,
        compiler_params=params,
        cost_estimate=pl.CostEstimate(flops=2**29, bytes_accessed=2**21, transcendentals=0),
        name="pick",
    )(place[:, None], mine, from_other)
    got = lax.all_to_all(sent, ("zh", "x"), 0, 0)

    entries = jnp.arange(coef_table.shape[0], dtype=I32)
    onehot = (cand_index[:, :, None] == entries[None, None, :]).astype(F32)
    coefficient = jnp.sum(onehot * coef_table[None, None, :], axis=2)
    return pl.pallas_call(
        decode_kernel,
        out_shape=jax.ShapeDtypeStruct((32, 4, width), BF16),
        in_specs=[pl.BlockSpec(memory_space=pltpu.SMEM), vmem],
        out_specs=vmem,
        compiler_params=params,
        scratch_shapes=[pltpu.VMEM((16, 32, 128), F32)] * 2,
        name="decode",
    )(coefficient, got)


def solution(mesh):
    fine = Mesh(mesh.devices.reshape(4, 4, 4, 4, 2), AXES)
    src, shard = ("x", "zh"), ("y", "zl", "c")
    placed = (P(src, None, shard), P(src + shard, None), P(), P(), P())
    return jax.shard_map(on_device, mesh=fine, in_specs=placed, out_specs=P(src, None, shard), check_vma=False)
```

```python
import jax
import jax.numpy as jnp
from jax import lax
from jax.experimental import pallas as pl
from jax.experimental.pallas import tpu as pltpu
from jax.sharding import Mesh, PartitionSpec as P

BF16, F32, I16, I32 = jnp.bfloat16, jnp.float32, jnp.int16, jnp.int32
LANES = 512
TOP = 32767.0
AXES = ("x", "zh", "y", "zl", "c")


def spread(block, axes):
    return lax.all_to_all(jnp.broadcast_to(block[None], (16,) + block.shape), axes, 0, 0)


def lines(first):
    return [[(i * 4 + k) * 2 + first for i in range(4)] for k in range(4)] + [
        [(k * 4 + i) * 2 + 1 - first for i in range(4)] for k in range(4)
    ]


def encode(partial, out_ref):
    rows, width = partial.shape
    main = LANES - 128
    top = jnp.max(jnp.abs(partial), axis=1, keepdims=True)
    power = jnp.clip(jnp.floor(jnp.log2(top)), -80.0, 80.0)
    mantissa = jnp.ceil(top * jnp.exp2(-power) * 8192.0) + 1.0
    per_step = 1.0 / (mantissa * jnp.exp2(power) * (1.0 / (8192.0 * TOP)))
    tail = jnp.concatenate([partial[:, main:], jnp.zeros((rows, LANES - width), F32)], axis=1)
    tail = jnp.round(tail * per_step)
    column = lax.broadcasted_iota(I32, (rows, 128), 1) + main
    tail = jnp.where(column == width, mantissa, jnp.where(column == width + 1, power, tail))
    for codes, columns in ((jnp.round(partial[:, :main] * per_step), slice(0, main)), (tail, slice(main, LANES))):
        high = jnp.floor(codes * (1.0 / 256.0))
        out_ref[:rows, columns] = high.astype(BF16)
        out_ref[rows:, columns] = (codes - high * 256.0).astype(BF16)


def times(rows, weights):
    return lax.dot_general(rows, weights, (((1,), (1,)), ((), ())), preferred_element_type=F32)


def picked(place, half, bytes_ref):
    found = place - half == lax.broadcasted_iota(I32, (place.shape[0], 256), 1)
    pick = jnp.concatenate([jnp.where(found, 256.0, 0.0), jnp.where(found, 1.0, 0.0)], axis=1).astype(BF16)
    return jnp.dot(pick, bytes_ref[...], preferred_element_type=F32)


def product(rows_ref, w_ref, far_ref, near_ref, arrived):
    pieces = arrived.shape[0]
    depth = far_ref.shape[1] // pieces
    copies = []
    for k in range(pieces):
        part = pl.ds(k * depth, depth)
        copies.append(pltpu.make_async_copy(far_ref.at[:, part], near_ref.at[:, part], arrived.at[k]))
        copies[k].start()
    total = None
    for k, copy in enumerate(copies):
        copy.wait()
        part = slice(k * depth, (k + 1) * depth)
        term = times(rows_ref[:, part], w_ref[:, part])
        total = term if k == 0 else total + term
    return total


def own_kernel(place_ref, rows_ref, far_ref, out_ref, w_ref, bytes_ref, arrived):
    encode(product(rows_ref, w_ref, far_ref, w_ref, arrived), bytes_ref)
    out_ref[...] = picked(place_ref[...], 0, bytes_ref)


def other_kernel(core_ref, place_ref, rows_ref, w_ref, own_ref, out_ref, bytes_ref):
    encode(times(rows_ref[...], w_ref[...]), bytes_ref)
    lane16, lane8 = lax.broadcasted_iota(I32, (16, 128), 1), lax.broadcasted_iota(I32, (8, 128), 1)
    for at in range(0, 512, 256):
        codes = own_ref[at : at + 256] + picked(place_ref[at : at + 256], 256, bytes_ref)
        for block in range(8):
            rows = codes[block * 32 : block * 32 + 32]
            tail = rows[:, 384:]
            fold = jnp.where(lane16 < 64, tail[:16], pltpu.roll(tail[16:], 64, 1))
            a, b, c, d = (pltpu.roll(tail[8 * i : 8 * i + 8], (64 + 32 * i) % 128, 1) for i in range(4))
            last = jnp.where(lane8 < 64, jnp.where(lane8 < 32, a, b), jnp.where(lane8 < 96, c, d))
            packed = jnp.concatenate([rows[:, :128], rows[:, 128:256], rows[:, 256:384], fold, last], axis=0)
            owner = at // 32 + block
            to = jnp.where(core_ref[0] == 0, owner, owner % 4 * 4 + owner // 4)
            out_ref[to] = packed.astype(I32).astype(I16)


def decode_kernel(coefficient_ref, got_ref, out_ref, tail_ref, step_ref):
    rows, cands, width = out_ref.shape
    lane = lax.broadcasted_iota(I32, (rows, 128), 1)
    at = width % 128
    for source in range(16):
        codes = got_ref[source, 96:].astype(I32).astype(F32)
        fold, last = codes[:16], codes[16:]
        folds = jnp.concatenate([fold, pltpu.roll(fold, 64, 1)], axis=0)
        lasts = jnp.concatenate([pltpu.roll(last, (64 - 32 * i) % 128, 1) for i in range(4)], axis=0)
        tail = jnp.where(lane < 64, folds, lasts)
        step = tail[:, at : at + 1] * jnp.exp2(tail[:, at + 1 : at + 2]) * (1.0 / (8192.0 * TOP))
        tail_ref[source] = tail * step
        step_ref[source] = jnp.broadcast_to(step, (rows, 128))
    for block in range(4):
        totals = [None] * cands
        for source in range(16):
            if block < 3:
                codes = got_ref[source, 32 * block : 32 * block + 32].astype(I32).astype(F32)
                values = codes * step_ref[source]
            else:
                values = tail_ref[source]
            for c in range(cands):
                term = coefficient_ref[c, source] * values
                totals[c] = term if source == 0 else totals[c] + term
        columns = slice(128 * block, min(128 * block + 128, width))
        stacked = jnp.stack([t[:, : columns.stop - columns.start] for t in totals], axis=1)
        out_ref[:, :, columns] = stacked.astype(BF16)


def on_device(weights, calib_pool, cand_index, coef_table, row_ids):
    core = lax.axis_index("c")
    w_piece = weights[0].T
    own = spread(calib_pool.reshape(32, 128), ("zh", "zl")).reshape(16, 4096)
    own = spread(own, ("x", "y")).reshape(256, 4096)
    other = lax.ppermute(own, "c", [(0, 1), (1, 0)])

    x, zh, y, zl, c = (row_ids >> 7) & 3, (row_ids >> 5) & 3, (row_ids >> 3) & 3, (row_ids >> 1) & 3, row_ids & 1
    place = (((x * 4 + y) * 4 + zh) * 4 + zl + jnp.where(c == core, 0, 256))[:, None]

    width = w_piece.shape[0]
    vmem, far = pl.BlockSpec(memory_space=pltpu.VMEM), pl.BlockSpec(memory_space=pltpu.HBM)
    params = pltpu.CompilerParams(vmem_limit_bytes=16 * 2**20)
    cost = pl.CostEstimate(flops=2 * 256 * 4096 * width, bytes_accessed=6 * 2**20, transcendentals=0)
    codes, w_here = pl.pallas_call(
        own_kernel,
        out_shape=(jax.ShapeDtypeStruct((512, LANES), F32), jax.ShapeDtypeStruct(w_piece.shape, BF16)),
        in_specs=[vmem, vmem, far],
        out_specs=(vmem, vmem),
        scratch_shapes=[pltpu.VMEM((512, LANES), BF16), pltpu.SemaphoreType.DMA((4,))],
        compiler_params=params,
        cost_estimate=cost,
        name="own",
    )(place, own, pltpu.with_memory_space_constraint(w_piece, pltpu.HBM))
    sent = pl.pallas_call(
        other_kernel,
        out_shape=jax.ShapeDtypeStruct((16, 120, 128), I16),
        in_specs=[pl.BlockSpec(memory_space=pltpu.SMEM)] + [vmem] * 4,
        out_specs=vmem,
        scratch_shapes=[pltpu.VMEM((512, LANES), BF16)],
        compiler_params=params,
        cost_estimate=cost,
        name="other",
    )(core.astype(I32)[None], place, other, w_here, codes)
    got = lax.all_to_all(sent.reshape(4, 4, 120, 128), ("x", "zh", "c"), 0, 0, axis_index_groups=lines(0))
    got = jnp.transpose(got, (1, 0, 2, 3))
    got = lax.all_to_all(got, ("x", "zh", "c"), 0, 0, axis_index_groups=lines(1)).reshape(16, 120, 128)

    entries = jnp.arange(coef_table.shape[0], dtype=I32)
    onehot = (cand_index[:, :, None] == entries[None, None, :]).astype(F32)
    coefficient = jnp.sum(onehot * coef_table[None, None, :], axis=2)
    turned = jnp.transpose(coefficient.reshape(4, 4, 4), (0, 2, 1)).reshape(4, 16)
    coefficient = jnp.where(core == 0, turned, coefficient)
    return pl.pallas_call(
        decode_kernel,
        out_shape=jax.ShapeDtypeStruct((32, 4, width), BF16),
        in_specs=[pl.BlockSpec(memory_space=pltpu.SMEM), vmem],
        out_specs=vmem,
        compiler_params=params,
        scratch_shapes=[pltpu.VMEM((16, 32, 128), F32)] * 2,
        name="decode",
    )(coefficient, got)


def solution(mesh):
    fine = Mesh(mesh.devices.reshape(4, 4, 4, 4, 2), AXES)
    src, shard = ("x", "zh"), ("y", "zl", "c")
    placed = (P(src, None, shard), P(src + shard, None), P(), P(), P())
    return jax.shard_map(on_device, mesh=fine, in_specs=placed, out_specs=P(src, None, shard), check_vma=False)
```

```python
import functools

import jax
import jax.numpy as jnp
from jax import lax
from jax.experimental import pallas as pl
from jax.experimental.pallas import tpu as pltpu
from jax.sharding import Mesh, PartitionSpec as P

BF16, F32, I16, I32 = jnp.bfloat16, jnp.float32, jnp.int16, jnp.int32
LANES = 512
TOP = 32767.0
AXES = ("x", "zh", "y", "zl", "c")


def spread(block, axes):
    return lax.all_to_all(jnp.broadcast_to(block[None], (16,) + block.shape), axes, 0, 0)


def lines(first):
    return [[(i * 4 + k) * 2 + first for i in range(4)] for k in range(4)] + [
        [(k * 4 + i) * 2 + 1 - first for i in range(4)] for k in range(4)
    ]


def encode(partial, out_ref):
    rows, width = partial.shape
    main = LANES - 128
    top = jnp.max(jnp.abs(partial), axis=1, keepdims=True)
    power = jnp.clip(jnp.floor(jnp.log2(top)), -80.0, 80.0)
    mantissa = jnp.ceil(top * jnp.exp2(-power) * 8192.0) + 1.0
    per_step = 1.0 / (mantissa * jnp.exp2(power) * (1.0 / (8192.0 * TOP)))
    tail = jnp.concatenate([partial[:, main:], jnp.zeros((rows, LANES - width), F32)], axis=1)
    tail = jnp.round(tail * per_step)
    column = lax.broadcasted_iota(I32, (rows, 128), 1) + main
    tail = jnp.where(column == width, mantissa, jnp.where(column == width + 1, power, tail))
    for codes, columns in ((jnp.round(partial[:, :main] * per_step), slice(0, main)), (tail, slice(main, LANES))):
        high = jnp.floor(codes * (1.0 / 256.0))
        out_ref[:rows, columns] = high.astype(BF16)
        out_ref[rows:, columns] = (codes - high * 256.0).astype(BF16)


def times(rows, weights):
    return lax.dot_general(rows, weights, (((1,), (1,)), ((), ())), preferred_element_type=F32)


def selection(place, half):
    found = place - half == lax.broadcasted_iota(I32, (place.shape[0], 256), 1)
    return jnp.concatenate([jnp.where(found, 256.0, 0.0), jnp.where(found, 1.0, 0.0)], axis=1).astype(BF16)


def product(rows_ref, w_ref, far_ref, near_ref, arrived, meanwhile=lambda: None):
    pieces = arrived.shape[0]
    depth = far_ref.shape[1] // pieces
    copies = []
    for k in range(pieces):
        part = pl.ds(k * depth, depth)
        copies.append(pltpu.make_async_copy(far_ref.at[:, part], near_ref.at[:, part], arrived.at[k]))
        copies[k].start()
    meanwhile()
    total = None
    for k, copy in enumerate(copies):
        copy.wait()
        part = slice(k * depth, (k + 1) * depth)
        term = times(rows_ref[:, part], w_ref[:, part])
        total = term if k == 0 else total + term
    return total


def own_kernel(place_ref, rows_ref, far_ref, out_ref, w_ref, bytes_ref, arrived):
    encode(product(rows_ref, w_ref, far_ref, w_ref, arrived), bytes_ref)
    out_ref[...] = jnp.dot(selection(place_ref[...], 0), bytes_ref[...], preferred_element_type=F32)


def store_selection(place_ref, pick_ref):
    pick_ref[...] = selection(place_ref[...], 256)


def other_kernel(core_ref, place_ref, far_ref, w_ref, own_ref, out_ref, rows_ref, bytes_ref, pick_ref, arrived):
    meanwhile = functools.partial(store_selection, place_ref, pick_ref)
    encode(product(rows_ref, w_ref, far_ref, rows_ref, arrived, meanwhile), bytes_ref)
    lane16, lane8 = lax.broadcasted_iota(I32, (16, 128), 1), lax.broadcasted_iota(I32, (8, 128), 1)
    for at in range(0, 512, 256):
        codes = own_ref[at : at + 256] + jnp.dot(
            pick_ref[at : at + 256], bytes_ref[...], preferred_element_type=F32
        )
        for block in range(8):
            rows = codes[block * 32 : block * 32 + 32]
            tail = rows[:, 384:]
            fold = jnp.where(lane16 < 64, tail[:16], pltpu.roll(tail[16:], 64, 1))
            a, b, c, d = (pltpu.roll(tail[8 * i : 8 * i + 8], (64 + 32 * i) % 128, 1) for i in range(4))
            last = jnp.where(lane8 < 64, jnp.where(lane8 < 32, a, b), jnp.where(lane8 < 96, c, d))
            packed = jnp.concatenate([rows[:, :128], rows[:, 128:256], rows[:, 256:384], fold, last], axis=0)
            owner = at // 32 + block
            to = jnp.where(core_ref[0] == 0, owner, owner % 4 * 4 + owner // 4)
            out_ref[to] = packed.astype(I32).astype(I16)


def turn_kernel(in_ref, out_ref):
    for a in range(4):
        for b in range(4):
            out_ref[b, a] = in_ref[a, b]


def decode_kernel(coefficient_ref, got_ref, out_ref, tail_ref, step_ref):
    rows, cands, width = out_ref.shape
    lane = lax.broadcasted_iota(I32, (rows, 128), 1)
    at = width % 128
    for source in range(16):
        codes = got_ref[source, 96:].astype(I32).astype(F32)
        fold, last = codes[:16], codes[16:]
        folds = jnp.concatenate([fold, pltpu.roll(fold, 64, 1)], axis=0)
        lasts = jnp.concatenate([pltpu.roll(last, (64 - 32 * i) % 128, 1) for i in range(4)], axis=0)
        tail = jnp.where(lane < 64, folds, lasts)
        step = tail[:, at : at + 1] * jnp.exp2(tail[:, at + 1 : at + 2]) * (1.0 / (8192.0 * TOP))
        tail_ref[source] = tail * step
        step_ref[source] = jnp.broadcast_to(step, (rows, 128))
    sums = []
    for block in range(4):
        totals = [None] * cands
        for source in range(16):
            if block < 3:
                codes = got_ref[source, 32 * block : 32 * block + 32].astype(I32).astype(F32)
                values = codes * step_ref[source]
            else:
                values = tail_ref[source]
            for c in range(cands):
                term = coefficient_ref[c, source] * values
                totals[c] = term if source == 0 else totals[c] + term
        sums.append(jnp.concatenate([t.astype(BF16) for t in totals], axis=0))
    to, of = (lax.broadcasted_iota(I32, (rows * cands, rows * cands), d) for d in (0, 1))
    order = jnp.where(to % cands * rows + to // cands == of, 1.0, 0.0).astype(BF16)
    laid = jnp.dot(order, jnp.concatenate(sums, axis=1)[:, :width], preferred_element_type=F32)
    out_ref[...] = laid.reshape(rows, cands, width).astype(BF16)


def on_device(weights, calib_pool, cand_index, coef_table, row_ids):
    core = lax.axis_index("c")
    w_piece = weights[0].T
    own = spread(calib_pool.reshape(32, 128), ("zh", "zl")).reshape(16, 4096)
    own = spread(own, ("x", "y")).reshape(256, 4096)
    other = lax.ppermute(own, "c", [(0, 1), (1, 0)])

    x, zh, y, zl, c = (row_ids >> 7) & 3, (row_ids >> 5) & 3, (row_ids >> 3) & 3, (row_ids >> 1) & 3, row_ids & 1
    place = (((x * 4 + y) * 4 + zh) * 4 + zl + jnp.where(c == core, 0, 256))[:, None]

    width = w_piece.shape[0]
    vmem, far = pl.BlockSpec(memory_space=pltpu.VMEM), pl.BlockSpec(memory_space=pltpu.HBM)
    params = pltpu.CompilerParams(vmem_limit_bytes=16 * 2**20)
    cost = pl.CostEstimate(flops=2 * 256 * 4096 * width, bytes_accessed=6 * 2**20, transcendentals=0)
    codes, w_here = pl.pallas_call(
        own_kernel,
        out_shape=(jax.ShapeDtypeStruct((512, LANES), F32), jax.ShapeDtypeStruct(w_piece.shape, BF16)),
        in_specs=[vmem, vmem, far],
        out_specs=(vmem, vmem),
        scratch_shapes=[pltpu.VMEM((512, LANES), BF16), pltpu.SemaphoreType.DMA((4,))],
        compiler_params=params,
        cost_estimate=cost,
        name="own",
    )(place, own, pltpu.with_memory_space_constraint(w_piece, pltpu.HBM))
    sent = pl.pallas_call(
        other_kernel,
        out_shape=jax.ShapeDtypeStruct((16, 120, 128), I16),
        in_specs=[pl.BlockSpec(memory_space=pltpu.SMEM), vmem, far, vmem, vmem],
        out_specs=vmem,
        scratch_shapes=[pltpu.VMEM((256, 4096), BF16)]
        + [pltpu.VMEM((512, LANES), BF16)] * 2
        + [pltpu.SemaphoreType.DMA((4,))],
        compiler_params=params,
        cost_estimate=cost,
        name="other",
    )(core.astype(I32)[None], place, pltpu.with_memory_space_constraint(other, pltpu.HBM), w_here, codes)
    got = lax.all_to_all(sent.reshape(4, 4, 120, 128), ("x", "zh", "c"), 0, 0, axis_index_groups=lines(0))
    got = pl.pallas_call(
        turn_kernel,
        out_shape=jax.ShapeDtypeStruct(got.shape, I16),
        in_specs=[vmem],
        out_specs=vmem,
        compiler_params=params,
        name="turn",
    )(got)
    got = lax.all_to_all(got, ("x", "zh", "c"), 0, 0, axis_index_groups=lines(1)).reshape(16, 120, 128)

    entries = jnp.arange(coef_table.shape[0], dtype=I32)
    onehot = (cand_index[:, :, None] == entries[None, None, :]).astype(F32)
    coefficient = jnp.sum(onehot * coef_table[None, None, :], axis=2)
    turned = jnp.transpose(coefficient.reshape(4, 4, 4), (0, 2, 1)).reshape(4, 16)
    coefficient = jnp.where(core == 0, turned, coefficient)
    return pl.pallas_call(
        decode_kernel,
        out_shape=jax.ShapeDtypeStruct((32, 4, width), BF16),
        in_specs=[pl.BlockSpec(memory_space=pltpu.SMEM), vmem],
        out_specs=vmem,
        compiler_params=params,
        scratch_shapes=[pltpu.VMEM((16, 32, 128), F32)] * 2,
        name="decode",
    )(coefficient, got)


def solution(mesh):
    fine = Mesh(mesh.devices.reshape(4, 4, 4, 4, 2), AXES)
    src, shard = ("x", "zh"), ("y", "zl", "c")
    placed = (P(src, None, shard), P(src + shard, None), P(), P(), P())
    return jax.shard_map(on_device, mesh=fine, in_specs=placed, out_specs=P(src, None, shard), check_vma=False)
```

```python
import functools

import jax
import jax.numpy as jnp
from jax import lax
from jax.experimental import pallas as pl
from jax.experimental.pallas import tpu as pltpu
from jax.sharding import Mesh, PartitionSpec as P

BF16, F32, I16, I32 = jnp.bfloat16, jnp.float32, jnp.int16, jnp.int32
LANES = 512
TOP = 32767.0
AXES = ("x", "zh", "y", "zl", "c")


def spread(block, axes, count, groups=None):
    copies = jnp.broadcast_to(block[None], (count,) + block.shape)
    return lax.all_to_all(copies, axes, 0, 0, axis_index_groups=groups)


def lines(first):
    return [[(i * 4 + k) * 2 + first for i in range(4)] for k in range(4)] + [
        [(k * 4 + i) * 2 + 1 - first for i in range(4)] for k in range(4)
    ]


def encode(partial, out_ref):
    rows, width = partial.shape
    main = LANES - 128
    top = jnp.max(jnp.abs(partial), axis=1, keepdims=True)
    power = jnp.clip(jnp.floor(jnp.log2(top)), -80.0, 80.0)
    mantissa = jnp.ceil(top * jnp.exp2(-power) * 8192.0) + 1.0
    per_step = 1.0 / (mantissa * jnp.exp2(power) * (1.0 / (8192.0 * TOP)))
    tail = jnp.concatenate([partial[:, main:], jnp.zeros((rows, LANES - width), F32)], axis=1)
    tail = jnp.round(tail * per_step)
    column = lax.broadcasted_iota(I32, (rows, 128), 1) + main
    tail = jnp.where(column == width, mantissa, jnp.where(column == width + 1, power, tail))
    for codes, columns in ((jnp.round(partial[:, :main] * per_step), slice(0, main)), (tail, slice(main, LANES))):
        high = jnp.floor(codes * (1.0 / 256.0))
        out_ref[:rows, columns] = high.astype(BF16)
        out_ref[rows:, columns] = (codes - high * 256.0).astype(BF16)


def times(rows, weights):
    return lax.dot_general(rows, weights, (((1,), (1,)), ((), ())), preferred_element_type=F32)


def selection(place, half):
    found = place - half == lax.broadcasted_iota(I32, (place.shape[0], 256), 1)
    return jnp.concatenate([jnp.where(found, 256.0, 0.0), jnp.where(found, 1.0, 0.0)], axis=1).astype(BF16)


def product(rows_ref, w_ref, far_ref, near_ref, arrived, meanwhile=lambda: None):
    pieces = arrived.shape[0]
    depth = far_ref.shape[1] // pieces
    copies = []
    for k in range(pieces):
        part = pl.ds(k * depth, depth)
        copies.append(pltpu.make_async_copy(far_ref.at[:, part], near_ref.at[:, part], arrived.at[k]))
        copies[k].start()
    meanwhile()
    total = None
    for k, copy in enumerate(copies):
        copy.wait()
        part = slice(k * depth, (k + 1) * depth)
        term = times(rows_ref[:, part], w_ref[:, part])
        total = term if k == 0 else total + term
    return total


def own_kernel(place_ref, rows_ref, far_ref, out_ref, w_ref, bytes_ref, arrived):
    encode(product(rows_ref, w_ref, far_ref, w_ref, arrived), bytes_ref)
    out_ref[...] = jnp.dot(selection(place_ref[...], 0), bytes_ref[...], preferred_element_type=F32)


def store_selection(place_ref, pick_ref):
    pick_ref[...] = selection(place_ref[...], 256)


def other_kernel(core_ref, place_ref, far_ref, w_ref, own_ref, out_ref, rows_ref, bytes_ref, pick_ref, arrived):
    meanwhile = functools.partial(store_selection, place_ref, pick_ref)
    encode(product(rows_ref, w_ref, far_ref, rows_ref, arrived, meanwhile), bytes_ref)
    lane16, lane8 = lax.broadcasted_iota(I32, (16, 128), 1), lax.broadcasted_iota(I32, (8, 128), 1)
    for at in range(0, 512, 256):
        codes = own_ref[at : at + 256] + jnp.dot(
            pick_ref[at : at + 256], bytes_ref[...], preferred_element_type=F32
        )
        for block in range(8):
            rows = codes[block * 32 : block * 32 + 32]
            tail = rows[:, 384:]
            fold = jnp.where(lane16 < 64, tail[:16], pltpu.roll(tail[16:], 64, 1))
            a, b, c, d = (pltpu.roll(tail[8 * i : 8 * i + 8], (64 + 32 * i) % 128, 1) for i in range(4))
            last = jnp.where(lane8 < 64, jnp.where(lane8 < 32, a, b), jnp.where(lane8 < 96, c, d))
            packed = jnp.concatenate([rows[:, :128], rows[:, 128:256], rows[:, 256:384], fold, last], axis=0)
            owner = at // 32 + block
            to = jnp.where(core_ref[0] == 0, owner, owner % 4 * 4 + owner // 4)
            out_ref[to] = packed.astype(I32).astype(I16)


def turn_kernel(in_ref, out_ref):
    for a in range(4):
        for b in range(4):
            out_ref[b, a] = in_ref[a, b]


def decode_kernel(coefficient_ref, got_ref, out_ref, tail_ref, step_ref):
    rows, cands, width = out_ref.shape
    lane = lax.broadcasted_iota(I32, (rows, 128), 1)
    at = width % 128
    for source in range(16):
        codes = got_ref[source, 96:].astype(I32).astype(F32)
        fold, last = codes[:16], codes[16:]
        folds = jnp.concatenate([fold, pltpu.roll(fold, 64, 1)], axis=0)
        lasts = jnp.concatenate([pltpu.roll(last, (64 - 32 * i) % 128, 1) for i in range(4)], axis=0)
        tail = jnp.where(lane < 64, folds, lasts)
        step = tail[:, at : at + 1] * jnp.exp2(tail[:, at + 1 : at + 2]) * (1.0 / (8192.0 * TOP))
        tail_ref[source] = tail * step
        step_ref[source] = jnp.broadcast_to(step, (rows, 128))
    sums = []
    for block in range(4):
        totals = [None] * cands
        for source in range(16):
            if block < 3:
                codes = got_ref[source, 32 * block : 32 * block + 32].astype(I32).astype(F32)
                values = codes * step_ref[source]
            else:
                values = tail_ref[source]
            for c in range(cands):
                term = coefficient_ref[c, source] * values
                totals[c] = term if source == 0 else totals[c] + term
        sums.append(jnp.concatenate([t.astype(BF16) for t in totals], axis=0))
    to, of = (lax.broadcasted_iota(I32, (rows * cands, rows * cands), d) for d in (0, 1))
    order = jnp.where(to % cands * rows + to // cands == of, 1.0, 0.0).astype(BF16)
    laid = jnp.dot(order, jnp.concatenate(sums, axis=1)[:, :width], preferred_element_type=F32)
    out_ref[...] = laid.reshape(rows, cands, width).astype(BF16)


def on_device(weights, calib_pool, cand_index, coef_table, row_ids):
    core = lax.axis_index("c")
    w_piece = weights[0].T
    own = spread(calib_pool.reshape(32, 128), ("zh", "zl"), 16).reshape(16, 4096)
    own = spread(own, ("x", "y", "c"), 4, lines(1)).reshape(64, 4096)
    own = spread(own, ("x", "y", "c"), 4, lines(0)).reshape(256, 4096)
    other = lax.ppermute(own, "c", [(0, 1), (1, 0)])

    x, zh, y, zl, c = (row_ids >> 7) & 3, (row_ids >> 5) & 3, (row_ids >> 3) & 3, (row_ids >> 1) & 3, row_ids & 1
    line = jnp.where(c == 0, x * 4 + y, y * 4 + x)
    place = ((line * 4 + zh) * 4 + zl + jnp.where(c == core, 0, 256))[:, None]

    width = w_piece.shape[0]
    vmem, far = pl.BlockSpec(memory_space=pltpu.VMEM), pl.BlockSpec(memory_space=pltpu.HBM)
    params = pltpu.CompilerParams(vmem_limit_bytes=16 * 2**20)
    cost = pl.CostEstimate(flops=2 * 256 * 4096 * width, bytes_accessed=6 * 2**20, transcendentals=0)
    codes, w_here = pl.pallas_call(
        own_kernel,
        out_shape=(jax.ShapeDtypeStruct((512, LANES), F32), jax.ShapeDtypeStruct(w_piece.shape, BF16)),
        in_specs=[vmem, vmem, far],
        out_specs=(vmem, vmem),
        scratch_shapes=[pltpu.VMEM((512, LANES), BF16), pltpu.SemaphoreType.DMA((4,))],
        compiler_params=params,
        cost_estimate=cost,
        name="own",
    )(place, own, pltpu.with_memory_space_constraint(w_piece, pltpu.HBM))
    sent = pl.pallas_call(
        other_kernel,
        out_shape=jax.ShapeDtypeStruct((16, 120, 128), I16),
        in_specs=[pl.BlockSpec(memory_space=pltpu.SMEM), vmem, far, vmem, vmem],
        out_specs=vmem,
        scratch_shapes=[pltpu.VMEM((256, 4096), BF16)]
        + [pltpu.VMEM((512, LANES), BF16)] * 2
        + [pltpu.SemaphoreType.DMA((4,))],
        compiler_params=params,
        cost_estimate=cost,
        name="other",
    )(core.astype(I32)[None], place, pltpu.with_memory_space_constraint(other, pltpu.HBM), w_here, codes)
    got = lax.all_to_all(sent.reshape(4, 4, 120, 128), ("x", "zh", "c"), 0, 0, axis_index_groups=lines(0))
    got = pl.pallas_call(
        turn_kernel,
        out_shape=jax.ShapeDtypeStruct(got.shape, I16),
        in_specs=[vmem],
        out_specs=vmem,
        compiler_params=params,
        name="turn",
    )(got)
    got = lax.all_to_all(got, ("x", "zh", "c"), 0, 0, axis_index_groups=lines(1)).reshape(16, 120, 128)

    entries = jnp.arange(coef_table.shape[0], dtype=I32)
    onehot = (cand_index[:, :, None] == entries[None, None, :]).astype(F32)
    coefficient = jnp.sum(onehot * coef_table[None, None, :], axis=2)
    turned = jnp.transpose(coefficient.reshape(4, 4, 4), (0, 2, 1)).reshape(4, 16)
    coefficient = jnp.where(core == 0, turned, coefficient)
    return pl.pallas_call(
        decode_kernel,
        out_shape=jax.ShapeDtypeStruct((32, 4, width), BF16),
        in_specs=[pl.BlockSpec(memory_space=pltpu.SMEM), vmem],
        out_specs=vmem,
        compiler_params=params,
        scratch_shapes=[pltpu.VMEM((16, 32, 128), F32)] * 2,
        name="decode",
    )(coefficient, got)


def solution(mesh):
    fine = Mesh(mesh.devices.reshape(4, 4, 4, 4, 2), AXES)
    src, shard = ("x", "zh"), ("y", "zl", "c")
    placed = (P(src, None, shard), P(src + shard, None), P(), P(), P())
    return jax.shard_map(on_device, mesh=fine, in_specs=placed, out_specs=P(src, None, shard), check_vma=False)
```

```python
import functools

import jax
import jax.numpy as jnp
from jax import lax
from jax.experimental import pallas as pl
from jax.experimental.pallas import tpu as pltpu
from jax.sharding import Mesh, PartitionSpec as P

BF16, F32, I16, I32 = jnp.bfloat16, jnp.float32, jnp.int16, jnp.int32
LANES = 512
TOP = 32767.0
AXES = ("x", "zh", "y", "zl", "c")


def spread(block, axes):
    return lax.all_to_all(jnp.broadcast_to(block[None], (16,) + block.shape), axes, 0, 0)


def lines(first):
    return [[(i * 4 + k) * 2 + first for i in range(4)] for k in range(4)] + [
        [(k * 4 + i) * 2 + 1 - first for i in range(4)] for k in range(4)
    ]


def encode(partial, out_ref):
    rows, width = partial.shape
    main = LANES - 128
    top = jnp.max(jnp.abs(partial), axis=1, keepdims=True)
    power = jnp.clip(jnp.floor(jnp.log2(top)), -80.0, 80.0)
    mantissa = jnp.ceil(top * jnp.exp2(-power) * 8192.0) + 1.0
    per_step = 1.0 / (mantissa * jnp.exp2(power) * (1.0 / (8192.0 * TOP)))
    tail = jnp.concatenate([partial[:, main:], jnp.zeros((rows, LANES - width), F32)], axis=1)
    tail = jnp.round(tail * per_step)
    column = lax.broadcasted_iota(I32, (rows, 128), 1) + main
    tail = jnp.where(column == width, mantissa, jnp.where(column == width + 1, power, tail))
    for codes, columns in ((jnp.round(partial[:, :main] * per_step), slice(0, main)), (tail, slice(main, LANES))):
        high = jnp.floor(codes * (1.0 / 256.0))
        out_ref[:rows, columns] = high.astype(BF16)
        out_ref[rows:, columns] = (codes - high * 256.0).astype(BF16)


def times(rows, weights):
    return lax.dot_general(rows, weights, (((1,), (1,)), ((), ())), preferred_element_type=F32)


def selection(place, half):
    found = place - half == lax.broadcasted_iota(I32, (place.shape[0], 256), 1)
    return jnp.concatenate([jnp.where(found, 256.0, 0.0), jnp.where(found, 1.0, 0.0)], axis=1).astype(BF16)


def product(rows_ref, w_ref, far_ref, near_ref, arrived, meanwhile=lambda: None):
    pieces = arrived.shape[0]
    depth = far_ref.shape[1] // pieces
    copies = []
    for k in range(pieces):
        part = pl.ds(k * depth, depth)
        copies.append(pltpu.make_async_copy(far_ref.at[:, part], near_ref.at[:, part], arrived.at[k]))
        copies[k].start()
    meanwhile()
    total = None
    for k, copy in enumerate(copies):
        copy.wait()
        part = slice(k * depth, (k + 1) * depth)
        term = times(rows_ref[:, part], w_ref[:, part])
        total = term if k == 0 else total + term
    return total


def own_kernel(place_ref, rows_ref, far_ref, out_ref, w_ref, bytes_ref, arrived):
    encode(product(rows_ref, w_ref, far_ref, w_ref, arrived), bytes_ref)
    out_ref[...] = jnp.dot(selection(place_ref[...], 0), bytes_ref[...], preferred_element_type=F32)


def store_selection(place_ref, pick_ref):
    pick_ref[...] = selection(place_ref[...], 256)


def other_kernel(core_ref, place_ref, far_ref, w_ref, own_ref, out_ref, rows_ref, bytes_ref, pick_ref, arrived):
    meanwhile = functools.partial(store_selection, place_ref, pick_ref)
    encode(product(rows_ref, w_ref, far_ref, rows_ref, arrived, meanwhile), bytes_ref)
    lane16, lane8 = lax.broadcasted_iota(I32, (16, 128), 1), lax.broadcasted_iota(I32, (8, 128), 1)
    for at in range(0, 512, 256):
        codes = own_ref[at : at + 256] + jnp.dot(
            pick_ref[at : at + 256], bytes_ref[...], preferred_element_type=F32
        )
        for block in range(8):
            rows = codes[block * 32 : block * 32 + 32]
            tail = rows[:, 384:]
            fold = jnp.where(lane16 < 64, tail[:16], pltpu.roll(tail[16:], 64, 1))
            a, b, c, d = (pltpu.roll(tail[8 * i : 8 * i + 8], (64 + 32 * i) % 128, 1) for i in range(4))
            last = jnp.where(lane8 < 64, jnp.where(lane8 < 32, a, b), jnp.where(lane8 < 96, c, d))
            packed = jnp.concatenate([rows[:, :128], rows[:, 128:256], rows[:, 256:384], fold, last], axis=0)
            owner = at // 32 + block
            to = jnp.where(core_ref[0] == 1, owner, owner % 4 * 4 + owner // 4)
            out_ref[to] = packed.astype(I32).astype(I16)


def turn_kernel(in_ref, out_ref):
    for a in range(4):
        for b in range(4):
            out_ref[b, a] = in_ref[a, b]


def decode_kernel(coefficient_ref, got_ref, out_ref, tail_ref, step_ref):
    rows, cands, width = out_ref.shape
    lane = lax.broadcasted_iota(I32, (rows, 128), 1)
    at = width % 128
    for source in range(16):
        codes = got_ref[source, 96:].astype(I32).astype(F32)
        fold, last = codes[:16], codes[16:]
        folds = jnp.concatenate([fold, pltpu.roll(fold, 64, 1)], axis=0)
        lasts = jnp.concatenate([pltpu.roll(last, (64 - 32 * i) % 128, 1) for i in range(4)], axis=0)
        tail = jnp.where(lane < 64, folds, lasts)
        step = tail[:, at : at + 1] * jnp.exp2(tail[:, at + 1 : at + 2]) * (1.0 / (8192.0 * TOP))
        tail_ref[source] = tail * step
        step_ref[source] = jnp.broadcast_to(step, (rows, 128))
    sums = []
    for block in range(4):
        totals = [None] * cands
        for source in range(16):
            if block < 3:
                codes = got_ref[source, 32 * block : 32 * block + 32].astype(I32).astype(F32)
                values = codes * step_ref[source]
            else:
                values = tail_ref[source]
            for c in range(cands):
                term = coefficient_ref[c, source] * values
                totals[c] = term if source == 0 else totals[c] + term
        sums.append(jnp.concatenate([t.astype(BF16) for t in totals], axis=0))
    to, of = (lax.broadcasted_iota(I32, (rows * cands, rows * cands), d) for d in (0, 1))
    order = jnp.where(to % cands * rows + to // cands == of, 1.0, 0.0).astype(BF16)
    laid = jnp.dot(order, jnp.concatenate(sums, axis=1)[:, :width], preferred_element_type=F32)
    out_ref[...] = laid.reshape(rows, cands, width).astype(BF16)


def on_device(weights, calib_pool, cand_index, coef_table, row_ids):
    core = lax.axis_index("c")
    w_piece = weights[0].T
    own = spread(calib_pool.reshape(32, 128), ("zh", "zl")).reshape(16, 4096)
    own = spread(own, ("x", "y")).reshape(256, 4096)
    other = lax.ppermute(own, "c", [(0, 1), (1, 0)])

    x, zh, y, zl, c = (row_ids >> 7) & 3, (row_ids >> 5) & 3, (row_ids >> 3) & 3, (row_ids >> 1) & 3, row_ids & 1
    place = (((x * 4 + y) * 4 + zh) * 4 + zl + jnp.where(c == core, 0, 256))[:, None]

    width = w_piece.shape[0]
    vmem, far = pl.BlockSpec(memory_space=pltpu.VMEM), pl.BlockSpec(memory_space=pltpu.HBM)
    params = pltpu.CompilerParams(vmem_limit_bytes=16 * 2**20)
    cost = pl.CostEstimate(flops=2 * 256 * 4096 * width, bytes_accessed=6 * 2**20, transcendentals=0)
    codes, w_here = pl.pallas_call(
        own_kernel,
        out_shape=(jax.ShapeDtypeStruct((512, LANES), F32), jax.ShapeDtypeStruct(w_piece.shape, BF16)),
        in_specs=[vmem, vmem, far],
        out_specs=(vmem, vmem),
        scratch_shapes=[pltpu.VMEM((512, LANES), BF16), pltpu.SemaphoreType.DMA((4,))],
        compiler_params=params,
        cost_estimate=cost,
        name="own",
    )(place, own, pltpu.with_memory_space_constraint(w_piece, pltpu.HBM))
    sent = pl.pallas_call(
        other_kernel,
        out_shape=jax.ShapeDtypeStruct((16, 120, 128), I16),
        in_specs=[pl.BlockSpec(memory_space=pltpu.SMEM), vmem, far, vmem, vmem],
        out_specs=vmem,
        scratch_shapes=[pltpu.VMEM((256, 4096), BF16)]
        + [pltpu.VMEM((512, LANES), BF16)] * 2
        + [pltpu.SemaphoreType.DMA((4,))],
        compiler_params=params,
        cost_estimate=cost,
        name="other",
    )(core.astype(I32)[None], place, pltpu.with_memory_space_constraint(other, pltpu.HBM), w_here, codes)
    got = lax.all_to_all(sent.reshape(4, 4, 120, 128), ("x", "zh", "c"), 0, 0, axis_index_groups=lines(1))
    got = pl.pallas_call(
        turn_kernel,
        out_shape=jax.ShapeDtypeStruct(got.shape, I16),
        in_specs=[vmem],
        out_specs=vmem,
        compiler_params=params,
        name="turn",
    )(got)
    got = lax.all_to_all(got, ("x", "zh", "c"), 0, 0, axis_index_groups=lines(0)).reshape(16, 120, 128)

    entries = jnp.arange(coef_table.shape[0], dtype=I32)
    onehot = (cand_index[:, :, None] == entries[None, None, :]).astype(F32)
    coefficient = jnp.sum(onehot * coef_table[None, None, :], axis=2)
    turned = jnp.transpose(coefficient.reshape(4, 4, 4), (0, 2, 1)).reshape(4, 16)
    coefficient = jnp.where(core == 1, turned, coefficient)
    return pl.pallas_call(
        decode_kernel,
        out_shape=jax.ShapeDtypeStruct((32, 4, width), BF16),
        in_specs=[pl.BlockSpec(memory_space=pltpu.SMEM), vmem],
        out_specs=vmem,
        compiler_params=params,
        scratch_shapes=[pltpu.VMEM((16, 32, 128), F32)] * 2,
        name="decode",
    )(coefficient, got)


def solution(mesh):
    fine = Mesh(mesh.devices.reshape(4, 4, 4, 4, 2), AXES)
    src, shard = ("x", "zh"), ("y", "zl", "c")
    placed = (P(src, None, shard), P(src + shard, None), P(), P(), P())
    return jax.shard_map(on_device, mesh=fine, in_specs=placed, out_specs=P(src, None, shard), check_vma=False)
```

```python
import functools

import jax
import jax.numpy as jnp
from jax import lax
from jax.experimental import pallas as pl
from jax.experimental.pallas import tpu as pltpu
from jax.sharding import Mesh, PartitionSpec as P

BF16, F32, I16, I32 = jnp.bfloat16, jnp.float32, jnp.int16, jnp.int32
LANES = 512
TOP = 32767.0
AXES = ("x", "zh", "y", "zl", "c")


def spread(block, axes, count, groups=None):
    copies = jnp.broadcast_to(block[None], (count,) + block.shape)
    return lax.all_to_all(copies, axes, 0, 0, axis_index_groups=groups)


def lines(first):
    return [[(i * 4 + k) * 2 + first for i in range(4)] for k in range(4)] + [
        [(k * 4 + i) * 2 + 1 - first for i in range(4)] for k in range(4)
    ]


def encode(partial, out_ref):
    rows, width = partial.shape
    main = LANES - 128
    top = jnp.max(jnp.abs(partial), axis=1, keepdims=True)
    power = jnp.clip(jnp.floor(jnp.log2(top)), -80.0, 80.0)
    mantissa = jnp.ceil(top * jnp.exp2(-power) * 8192.0) + 1.0
    per_step = 1.0 / (mantissa * jnp.exp2(power) * (1.0 / (8192.0 * TOP)))
    tail = jnp.concatenate([partial[:, main:], jnp.zeros((rows, LANES - width), F32)], axis=1)
    tail = jnp.round(tail * per_step)
    column = lax.broadcasted_iota(I32, (rows, 128), 1) + main
    tail = jnp.where(column == width, mantissa, jnp.where(column == width + 1, power, tail))
    for codes, columns in ((jnp.round(partial[:, :main] * per_step), slice(0, main)), (tail, slice(main, LANES))):
        high = jnp.floor(codes * (1.0 / 256.0))
        out_ref[:rows, columns] = high.astype(BF16)
        out_ref[rows:, columns] = (codes - high * 256.0).astype(BF16)


def times(rows, weights):
    return lax.dot_general(rows, weights, (((1,), (1,)), ((), ())), preferred_element_type=F32)


def selection(place, half):
    found = place - half == lax.broadcasted_iota(I32, (place.shape[0], 256), 1)
    return jnp.concatenate([jnp.where(found, 256.0, 0.0), jnp.where(found, 1.0, 0.0)], axis=1).astype(BF16)


def product(rows_ref, w_ref, far_ref, near_ref, arrived, meanwhile=lambda: None):
    pieces = arrived.shape[0]
    depth = far_ref.shape[1] // pieces
    copies = []
    for k in range(pieces):
        part = pl.ds(k * depth, depth)
        copies.append(pltpu.make_async_copy(far_ref.at[:, part], near_ref.at[:, part], arrived.at[k]))
        copies[k].start()
    meanwhile()
    total = None
    for k, copy in enumerate(copies):
        copy.wait()
        part = slice(k * depth, (k + 1) * depth)
        term = times(rows_ref[:, part], w_ref[:, part])
        total = term if k == 0 else total + term
    return total


def own_kernel(place_ref, rows_ref, far_ref, out_ref, w_ref, bytes_ref, arrived):
    encode(product(rows_ref, w_ref, far_ref, w_ref, arrived), bytes_ref)
    out_ref[...] = jnp.dot(selection(place_ref[...], 0), bytes_ref[...], preferred_element_type=F32)


def store_selection(place_ref, pick_ref):
    pick_ref[...] = selection(place_ref[...], 256)


def other_kernel(core_ref, place_ref, far_ref, w_ref, own_ref, out_ref, rows_ref, bytes_ref, pick_ref, arrived):
    meanwhile = functools.partial(store_selection, place_ref, pick_ref)
    encode(product(rows_ref, w_ref, far_ref, rows_ref, arrived, meanwhile), bytes_ref)
    lane16, lane8 = lax.broadcasted_iota(I32, (16, 128), 1), lax.broadcasted_iota(I32, (8, 128), 1)
    for at in range(0, 512, 256):
        codes = own_ref[at : at + 256] + jnp.dot(
            pick_ref[at : at + 256], bytes_ref[...], preferred_element_type=F32
        )
        for block in range(8):
            rows = codes[block * 32 : block * 32 + 32]
            tail = rows[:, 384:]
            fold = jnp.where(lane16 < 64, tail[:16], pltpu.roll(tail[16:], 64, 1))
            a, b, c, d = (pltpu.roll(tail[8 * i : 8 * i + 8], (64 + 32 * i) % 128, 1) for i in range(4))
            last = jnp.where(lane8 < 64, jnp.where(lane8 < 32, a, b), jnp.where(lane8 < 96, c, d))
            packed = jnp.concatenate([rows[:, :128], rows[:, 128:256], rows[:, 256:384], fold, last], axis=0)
            owner = at // 32 + block
            to = jnp.where(core_ref[0] == 0, owner, owner % 4 * 4 + owner // 4)
            out_ref[to] = packed.astype(I32).astype(I16)


def turn_kernel(in_ref, out_ref):
    for a in range(4):
        for b in range(4):
            out_ref[b, a] = in_ref[a, b]


def decode_kernel(coefficient_ref, got_ref, out_ref, tail_ref, step_ref):
    rows, cands, width = out_ref.shape
    lane = lax.broadcasted_iota(I32, (rows, 128), 1)
    at = width % 128
    for source in range(16):
        codes = got_ref[source, 96:].astype(I32).astype(F32)
        fold, last = codes[:16], codes[16:]
        folds = jnp.concatenate([fold, pltpu.roll(fold, 64, 1)], axis=0)
        lasts = jnp.concatenate([pltpu.roll(last, (64 - 32 * i) % 128, 1) for i in range(4)], axis=0)
        tail = jnp.where(lane < 64, folds, lasts)
        step = tail[:, at : at + 1] * jnp.exp2(tail[:, at + 1 : at + 2]) * (1.0 / (8192.0 * TOP))
        tail_ref[source] = tail * step
        step_ref[source] = jnp.broadcast_to(step, (rows, 128))
    sums = []
    for block in range(4):
        totals = [None] * cands
        for source in range(16):
            if block < 3:
                codes = got_ref[source, 32 * block : 32 * block + 32].astype(I32).astype(F32)
                values = codes * step_ref[source]
            else:
                values = tail_ref[source]
            for c in range(cands):
                term = coefficient_ref[c, source] * values
                totals[c] = term if source == 0 else totals[c] + term
        sums.append(jnp.concatenate([t.astype(BF16) for t in totals], axis=0))
    to, of = (lax.broadcasted_iota(I32, (rows * cands, rows * cands), d) for d in (0, 1))
    order = jnp.where(to % cands * rows + to // cands == of, 1.0, 0.0).astype(BF16)
    laid = jnp.dot(order, jnp.concatenate(sums, axis=1)[:, :width], preferred_element_type=F32)
    out_ref[...] = laid.reshape(rows, cands, width).astype(BF16)


def on_device(weights, calib_pool, cand_index, coef_table, row_ids):
    core = lax.axis_index("c")
    w_piece = weights[0].T
    own = spread(calib_pool.reshape(32, 128), ("zh", "zl"), 16).reshape(16, 4096)
    own = spread(own, ("x", "y", "c"), 4, lines(0)).reshape(64, 4096)
    own = spread(own, ("x", "y", "c"), 4, lines(1)).reshape(256, 4096)
    other = lax.ppermute(own, "c", [(0, 1), (1, 0)])

    x, zh, y, zl, c = (row_ids >> 7) & 3, (row_ids >> 5) & 3, (row_ids >> 3) & 3, (row_ids >> 1) & 3, row_ids & 1
    line = jnp.where(c == 1, x * 4 + y, y * 4 + x)
    place = ((line * 4 + zh) * 4 + zl + jnp.where(c == core, 0, 256))[:, None]

    width = w_piece.shape[0]
    vmem, far = pl.BlockSpec(memory_space=pltpu.VMEM), pl.BlockSpec(memory_space=pltpu.HBM)
    params = pltpu.CompilerParams(vmem_limit_bytes=16 * 2**20)
    cost = pl.CostEstimate(flops=2 * 256 * 4096 * width, bytes_accessed=6 * 2**20, transcendentals=0)
    codes, w_here = pl.pallas_call(
        own_kernel,
        out_shape=(jax.ShapeDtypeStruct((512, LANES), F32), jax.ShapeDtypeStruct(w_piece.shape, BF16)),
        in_specs=[vmem, vmem, far],
        out_specs=(vmem, vmem),
        scratch_shapes=[pltpu.VMEM((512, LANES), BF16), pltpu.SemaphoreType.DMA((4,))],
        compiler_params=params,
        cost_estimate=cost,
        name="own",
    )(place, own, pltpu.with_memory_space_constraint(w_piece, pltpu.HBM))
    sent = pl.pallas_call(
        other_kernel,
        out_shape=jax.ShapeDtypeStruct((16, 120, 128), I16),
        in_specs=[pl.BlockSpec(memory_space=pltpu.SMEM), vmem, far, vmem, vmem],
        out_specs=vmem,
        scratch_shapes=[pltpu.VMEM((256, 4096), BF16)]
        + [pltpu.VMEM((512, LANES), BF16)] * 2
        + [pltpu.SemaphoreType.DMA((4,))],
        compiler_params=params,
        cost_estimate=cost,
        name="other",
    )(core.astype(I32)[None], place, pltpu.with_memory_space_constraint(other, pltpu.HBM), w_here, codes)
    got = lax.all_to_all(sent.reshape(4, 4, 120, 128), ("x", "zh", "c"), 0, 0, axis_index_groups=lines(0))
    got = pl.pallas_call(
        turn_kernel,
        out_shape=jax.ShapeDtypeStruct(got.shape, I16),
        in_specs=[vmem],
        out_specs=vmem,
        compiler_params=params,
        name="turn",
    )(got)
    got = lax.all_to_all(got, ("x", "zh", "c"), 0, 0, axis_index_groups=lines(1)).reshape(16, 120, 128)

    entries = jnp.arange(coef_table.shape[0], dtype=I32)
    onehot = (cand_index[:, :, None] == entries[None, None, :]).astype(F32)
    coefficient = jnp.sum(onehot * coef_table[None, None, :], axis=2)
    turned = jnp.transpose(coefficient.reshape(4, 4, 4), (0, 2, 1)).reshape(4, 16)
    coefficient = jnp.where(core == 0, turned, coefficient)
    return pl.pallas_call(
        decode_kernel,
        out_shape=jax.ShapeDtypeStruct((32, 4, width), BF16),
        in_specs=[pl.BlockSpec(memory_space=pltpu.SMEM), vmem],
        out_specs=vmem,
        compiler_params=params,
        scratch_shapes=[pltpu.VMEM((16, 32, 128), F32)] * 2,
        name="decode",
    )(coefficient, got)


def solution(mesh):
    fine = Mesh(mesh.devices.reshape(4, 4, 4, 4, 2), AXES)
    src, shard = ("x", "zh"), ("y", "zl", "c")
    placed = (P(src, None, shard), P(src + shard, None), P(), P(), P())
    return jax.shard_map(on_device, mesh=fine, in_specs=placed, out_specs=P(src, None, shard), check_vma=False)
```
